256 devices in a mesh: segment: 2 (over core), tile: 128 (over x, y, z).
Axes of the slice: x: 4, y: 4, z: 8, core: 2. Of those that a mesh axis runs over, the one named last changes fastest.
Arguments:
- inputs: bfloat16 [2, 1024, 8, 256], P(None, 'tile'), may hold values from -6 to 6
- cotangent: bfloat16 [2, 1024, 8, 256], P(None, 'tile'), may hold values from -6 to 6
- side_owner: int32 [128, 4], replicated, may hold values from 0 to 127, as said below
- side_from: int32 [128, 4], replicated, may hold values from 0 to 3
- corner_from: int32 [128, 4], replicated, may hold values from 0 to 3
- corner_live: int32 [128, 4], replicated, may hold values 0 or 1
- depth_kernel: bfloat16 [4, 49, 256], P('segment'), may hold values from -0.875 to 0.875
- norm_gain: float32 [4, 256], P('segment'), may hold values from 0.1 to 1.9
- in_weight: bfloat16 [4, 256, 1024], P('segment'), may hold values from -0.375 to 0.375
- out_weight: bfloat16 [4, 1024, 256], P('segment'), may hold values from -0.1875 to 0.1875
- layer_scale: float32 [4, 256], P('segment'), may hold values from 0.1 to 1.9
Outputs:
- input_grads: bfloat16 [2, 1024, 8, 256], P('segment', 'tile')
- grad_kernel: float32 [4, 49, 256], P('segment')
- grad_gain: float32 [4, 256], P('segment')
- grad_in: float32 [4, 256, 1024], P('segment')
- grad_out: float32 [4, 1024, 256], P('segment')
- grad_scale: float32 [4, 256], P('segment')
The draws below stay inside these ranges and needn't reach their ends.
Inputs may be any that keep to these rules, and one draw needn't show every extreme that they name: side_owner[t,0] is t - 8 or t - 7, side_owner[t,1] is t + 1, side_owner[t,2] is t + 8 or t + 7, side_owner[t,3] is t - 1, all modulo 128.
All inputs are finite; a program needn't handle non-finite values.
Results may differ from the reference program's by a relative error of at most 0.024.
Values may be sent and summed in bfloat16 or wider, within the bound.
A program may use at most 128 MiB of HBM per device.

```python
import jax
import jax.numpy as jnp
from jax import lax

C = 256
HID = 1024
P_SIZE = 8
GW = 8
MB = 2
TILES = 128
BLOCKS = 4


def draw_side_owner(key, part):
    key = jax.random.fold_in(key, 17)
    key_north, key_south = jax.random.split(key)
    places = jnp.arange(TILES, dtype=jnp.int32)
    north_step = jax.random.randint(key_north, (TILES,), 0, 2, dtype=jnp.int32)
    south_step = jax.random.randint(key_south, (TILES,), 0, 2, dtype=jnp.int32)
    north_tile = (places - GW + north_step) % TILES
    east_tile = (places + 1) % TILES
    south_tile = (places + GW - south_step) % TILES
    west_tile = (places - 1) % TILES
    return jnp.stack([north_tile, east_tile, south_tile, west_tile], axis=1).astype(jnp.int32)


def set_ends(array, stream_key, low, largest):
    index_at = [jax.random.randint(jax.random.fold_in(stream_key, axis), (), 0, length) for axis, length in enumerate(array.shape)]
    longest = array.shape.index(max(array.shape))
    neighbour = index_at[:longest] + [(index_at[longest] + 1) % array.shape[longest]] + index_at[longest + 1:]
    return array.at[tuple(index_at)].set(low).at[tuple(neighbour)].set(largest)


def steps_of(key, extent, cuts, smallest, high):
    gain, own = 1.0, jax.random.fold_in(key, 6)
    for axis_at, blocks in cuts:
        heights = jnp.exp(jax.random.uniform(jax.random.fold_in(own, axis_at), (blocks,), jnp.float32, smallest / len(cuts), high / len(cuts)))
        gain = gain * jnp.repeat(heights, extent[axis_at] // blocks).reshape([-1 if axis == axis_at else 1 for axis in range(len(extent))])
    return gain


def normal_values(rng, dims, deviation, limit, cuts=(), kind=jnp.bfloat16):
    values = deviation * jax.random.normal(rng, dims, jnp.float32)
    if cuts:
        values = values * steps_of(rng, dims, cuts, -0.22, 0.18)
    return jnp.clip(values, -limit, limit).astype(kind)


def setup_inputs(seed: int = 0) -> dict:
    splits = jax.random.split(jax.random.key(seed), 12)
    return {
        "inputs": normal_values(splits[0], (MB, TILES * P_SIZE, P_SIZE, C), 1.0, 6.0, ((1, 128),)),
        "cotangent": normal_values(splits[1], (MB, TILES * P_SIZE, P_SIZE, C), 1.0, 6.0, ((1, 128),)),
        "side_owner": draw_side_owner(jax.random.fold_in(splits[11], 71), 0),
        "side_from": set_ends(jax.random.randint(splits[3], (TILES, 4), 0, 4), jax.random.fold_in(splits[3], 1), 0, 3).astype(jnp.int32),
        "corner_from": set_ends(jax.random.randint(splits[4], (TILES, 4), 0, 4), jax.random.fold_in(splits[4], 1), 0, 3).astype(jnp.int32),
        "corner_live": set_ends((jax.random.randint(splits[5], (TILES, 4), 0, 8) < 7).astype(jnp.int32), jax.random.fold_in(splits[5], 1), 0, 1),
        "depth_kernel": normal_values(splits[6], (BLOCKS, 49, C), 49 ** -0.5, 0.875, ((0, 2),)),
        "norm_gain": jnp.clip(1.0 + 0.18 * jax.random.normal(splits[7], (BLOCKS, C), jnp.float32), 0.1, 1.9),
        "in_weight": normal_values(splits[8], (BLOCKS, C, HID), C ** -0.5, 0.375, ((0, 2),)),
        "out_weight": normal_values(splits[9], (BLOCKS, HID, C), HID ** -0.5, 0.1875, ((0, 2),)),
        "layer_scale": jnp.clip(1.0 + 0.18 * jax.random.normal(splits[10], (BLOCKS, C), jnp.float32), 0.1, 1.9),
    }


EPSILON = 1e-06
ROOT_HALF = 0.7071067811865476
INV_ROOT_TAU = 0.3989422804014327

def depthwise(padded, weights):
    inner_size = padded.shape[-2] - 6
    summed = jnp.zeros(padded.shape[:-3] + (inner_size, inner_size, padded.shape[-1]), jnp.float32)
    for row_shift in range(7):
        for col_shift in range(7):
            window = padded[..., row_shift:row_shift + inner_size, col_shift:col_shift + inner_size, :]
            summed = summed + window * weights[row_shift * 7 + col_shift]
    return summed

def block_forward(padded, depth_kernel, norm_gain, in_weight, out_weight, layer_scale):
    channels = padded.shape[-1]
    filtered = depthwise(padded, depth_kernel.astype(jnp.float32))
    centred = filtered - lax.optimization_barrier(jnp.mean(filtered, axis=-1, keepdims=True))
    inv_std = lax.rsqrt(lax.optimization_barrier(jnp.mean(centred * centred, axis=-1, keepdims=True)) + EPSILON)
    normed = centred * inv_std
    unit_rows = (normed * norm_gain).astype(jnp.bfloat16).reshape(-1, channels)
    before = jnp.dot(unit_rows, in_weight, preferred_element_type=jnp.float32)
    hidden = jax.nn.gelu(before, approximate=False).astype(jnp.bfloat16)
    mixed_out = jnp.dot(hidden, out_weight, preferred_element_type=jnp.float32).reshape(filtered.shape)
    output = (padded[..., 3:-3, 3:-3, :] + layer_scale * mixed_out).astype(jnp.bfloat16)
    return (output, (normed, inv_std, unit_rows, before, hidden, mixed_out))

def block_backward(padded, kept_parts, upstream, depth_kernel, norm_gain, in_weight, out_weight, layer_scale):
    normed, inv_std, unit_rows, before, hidden, mixed_out = kept_parts
    channels = padded.shape[-1]
    inner_size = padded.shape[-2] - 6
    upper_grad = upstream.astype(jnp.float32)
    d_scale = lax.optimization_barrier(jnp.sum((upper_grad * mixed_out).reshape(-1, channels), axis=0))
    d_mixed = (upper_grad * layer_scale).astype(jnp.bfloat16).reshape(-1, channels)
    d_out = jnp.dot(hidden.T, d_mixed, preferred_element_type=jnp.float32)
    d_hidden = jnp.dot(d_mixed, out_weight.T, preferred_element_type=jnp.float32)
    slope = 0.5 * (1.0 + lax.erf(before * ROOT_HALF)) + before * jnp.exp(-0.5 * before * before) * INV_ROOT_TAU
    d_before = (d_hidden * slope).astype(jnp.bfloat16)
    d_in = jnp.dot(unit_rows.T, d_before, preferred_element_type=jnp.float32)
    d_unit = jnp.dot(d_before, in_weight.T, preferred_element_type=jnp.float32).reshape(normed.shape)
    d_gain = lax.optimization_barrier(jnp.sum((d_unit * normed).reshape(-1, channels), axis=0))
    d_normed = d_unit * norm_gain
    d_filtered = inv_std * (d_normed - lax.optimization_barrier(jnp.mean(d_normed, axis=-1, keepdims=True)) - normed * lax.optimization_barrier(jnp.mean(d_normed * normed, axis=-1, keepdims=True)))
    weights = depth_kernel.astype(jnp.float32)
    kernel_rows = []
    for row_shift in range(7):
        for col_shift in range(7):
            window = padded[..., row_shift:row_shift + inner_size, col_shift:col_shift + inner_size, :]
            kernel_rows.append(lax.optimization_barrier(jnp.sum((d_filtered * window).reshape(-1, channels), axis=0)))
    d_kernel = jnp.stack(kernel_rows)
    spread = [(0, 0)] * (d_filtered.ndim - 3) + [(6, 6), (6, 6), (0, 0)]
    d_padded = depthwise(jnp.pad(d_filtered, spread), weights[::-1])
    return (upper_grad, d_padded, (d_kernel, d_gain, d_in, d_out, d_scale))

def rim_set(tiles):
    return jnp.stack([jnp.rot90(tiles, quarter, axes=(-3, -2))[..., :3, :, :] for quarter in range(4)])

def put_patch(padded, patch_in, quarter, corner):
    turned = jnp.rot90(padded, quarter, axes=(-3, -2))
    if corner:
        turned = turned.at[..., 0:3, 0:3, :].set(patch_in)
    else:
        turned = turned.at[..., 0:3, 3:-3, :].set(patch_in)
    return jnp.rot90(turned, -quarter, axes=(-3, -2))

def take_patch(d_padded, quarter, corner):
    turned = jnp.rot90(d_padded, quarter, axes=(-3, -2))
    return turned[..., 0:3, 0:3, :] if corner else turned[..., 0:3, 3:-3, :]

def rims_to_tile(d_rims):
    inner_size = d_rims.shape[-2]
    summed = jnp.zeros(d_rims.shape[1:-3] + (inner_size, inner_size, d_rims.shape[-1]), d_rims.dtype)
    for quarter in range(4):
        filler = jnp.zeros(d_rims.shape[1:-3] + (inner_size - 3, inner_size, d_rims.shape[-1]), d_rims.dtype)
        extended = jnp.concatenate([d_rims[quarter], filler], axis=-3)
        summed = summed + jnp.rot90(extended, -quarter, axes=(-3, -2))
    return summed

def corner_owners(side_owner, tile_count):
    north_tile = side_owner[:, 0]
    south_tile = side_owner[:, 2]
    return [(north_tile - 1) % tile_count, (north_tile + 1) % tile_count, (south_tile + 1) % tile_count, (south_tile - 1) % tile_count]

def assemble(tiles, side_owner, side_from, corner_from, corner_live):
    tile_count = tiles.shape[1]
    rim_stack = rim_set(tiles)
    padded = jnp.pad(tiles, ((0, 0), (0, 0), (3, 3), (3, 3), (0, 0)))
    for side_at in range(4):
        pieces = jnp.moveaxis(rim_stack[side_from[:, side_at], :, side_owner[:, side_at]], 0, 1)
        padded = put_patch(padded, jnp.flip(pieces, (-3, -2)), side_at, False)
    owners = corner_owners(side_owner, tile_count)
    for corner in range(4):
        pieces = jnp.moveaxis(rim_stack[corner_from[:, corner], :, owners[corner]], 0, 1)[..., :3, :]
        pieces = pieces * corner_live[:, corner][None, :, None, None, None].astype(jnp.bfloat16)
        padded = put_patch(padded, jnp.flip(pieces, (-3, -2)), corner, True)
    return padded

def scatter_back(d_padded, side_owner, side_from, corner_from, corner_live):
    tile_count = d_padded.shape[1]
    inner_size = d_padded.shape[-2] - 6
    channels = d_padded.shape[-1]
    d_rims = jnp.zeros((4,) + d_padded.shape[:2] + (3, inner_size, channels), jnp.float32)
    for side_at in range(4):
        pieces = jnp.flip(take_patch(d_padded, side_at, False), (-3, -2))
        d_rims = d_rims.at[side_from[:, side_at], :, side_owner[:, side_at]].add(jnp.moveaxis(pieces, 1, 0))
    owners = corner_owners(side_owner, tile_count)
    for corner in range(4):
        pieces = jnp.flip(take_patch(d_padded, corner, True), (-3, -2))
        pieces = pieces * corner_live[:, corner][None, :, None, None, None].astype(jnp.float32)
        filler = jnp.zeros(pieces.shape[:-2] + (inner_size - 3, channels), jnp.float32)
        pieces = jnp.concatenate([pieces, filler], axis=-2)
        d_rims = d_rims.at[corner_from[:, corner], :, owners[corner]].add(jnp.moveaxis(pieces, 1, 0))
    return d_padded[..., 3:-3, 3:-3, :] + rims_to_tile(d_rims)

def reference(inputs, cotangent, side_owner, side_from, corner_from, corner_live, depth_kernel, norm_gain, in_weight, out_weight, layer_scale):
    current = inputs.reshape(MB, TILES, P_SIZE, P_SIZE, C)
    saved_pads = []
    for layer_at in range(BLOCKS):
        padded = assemble(current, side_owner, side_from, corner_from, corner_live)
        saved_pads.append(padded)
        current, unused = block_forward(padded.astype(jnp.float32), depth_kernel[layer_at], norm_gain[layer_at], in_weight[layer_at], out_weight[layer_at], layer_scale[layer_at])
    upstream = cotangent.reshape(MB, TILES, P_SIZE, P_SIZE, C)
    collected = [None] * BLOCKS
    for layer_at in reversed(range(BLOCKS)):
        padded = saved_pads[layer_at].astype(jnp.float32)
        unused, kept_parts = block_forward(padded, depth_kernel[layer_at], norm_gain[layer_at], in_weight[layer_at], out_weight[layer_at], layer_scale[layer_at])
        upper_grad, d_padded, grad_terms = block_backward(padded, kept_parts, upstream, depth_kernel[layer_at], norm_gain[layer_at], in_weight[layer_at], out_weight[layer_at], layer_scale[layer_at])
        d_input = upper_grad + scatter_back(d_padded, side_owner, side_from, corner_from, corner_live)
        upstream = d_input.astype(jnp.bfloat16)
        collected[layer_at] = grad_terms
    factor = (MB * TILES * P_SIZE * P_SIZE) ** (-0.5)
    grads = [jnp.stack([collected[layer_at][member] for layer_at in range(BLOCKS)]) * factor for member in range(5)]
    return (upstream.reshape(MB, TILES * P_SIZE, P_SIZE, C), grads[0], grads[1], grads[2], grads[3], grads[4])
```

```python
import functools

import jax
import jax.numpy as jnp
from jax import lax
from jax.experimental import pallas as pl
from jax.experimental.pallas import tpu as pltpu
from jax.sharding import PartitionSpec as P

GW = 8
BLOCKS = 4
C = 256
HID = 1024
EPSILON = 1e-06
ROOT_HALF = 0.7071067811865476
INV_ROOT_TAU = 0.3989422804014327
MESH = pl.DeviceIdType.MESH
F32 = jnp.float32
BF16 = jnp.bfloat16

OFFSETS = (-1, 1, -GW - 1, -GW, -GW + 1, -GW + 2, GW + 1, GW, GW - 1, GW - 2)
ROWS = (32, 32, 16, 32, 32, 16, 16, 32, 32, 16)
BASE = (0, 32, 192, 64, 96, 208, 224, 128, 160, 240)
SEND_ORDER = (2, 5, 6, 9, 3, 4, 7, 8, 0, 1)
SMALL = 56


def dot(a, b, da=1, db=0):
    return lax.dot_general(a, b, (((da,), (db,)), ((), ())), preferred_element_type=F32)


def pick(code, values):
    out = jnp.int32(values[-1])
    for k in range(len(values) - 2, -1, -1):
        out = jnp.where(code == k, jnp.int32(values[k]), out)
    return out


def seam_steps(so, t, n):
    north = lax.rem(so[t, 0] - t + GW + n, n)
    south = lax.rem(t + GW - so[t, 2] + n, n)
    return north, south


def wanted_rim(slot, t, so, sf, cf, n):
    north, south = seam_steps(so, t, n)
    if slot == 0:
        return sf[t, 3]
    if slot == 1:
        return sf[t, 1]
    if slot == 2:
        return cf[t, 0]
    if slot == 3:
        return jnp.where(north == 0, sf[t, 0], cf[t, 0])
    if slot == 4:
        return jnp.where(north == 1, sf[t, 0], cf[t, 1])
    if slot == 5:
        return cf[t, 1]
    if slot == 6:
        return cf[t, 2]
    if slot == 7:
        return jnp.where(south == 0, sf[t, 2], cf[t, 2])
    if slot == 8:
        return jnp.where(south == 1, sf[t, 2], cf[t, 3])
    return cf[t, 3]


def send_matrix(me, n, so, sf, cf):
    parts = [None] * 10
    for slot in range(10):
        rows = ROWS[slot]
        code = wanted_rim(slot, lax.rem(me - OFFSETS[slot] + n, n), so, sf, cf, n)
        a = pick(code, (0, 7, 63, 56))
        b = pick(code, (8, -1, -8, 1))
        d = pick(code, (1, 8, -1, -8))
        row = lax.broadcasted_iota(jnp.int32, (rows, 64), 0)
        pixel = lax.broadcasted_iota(jnp.int32, (rows, 64), 1)
        if rows == 32:
            i, j = row >> 3, row & 7
            valid = row < 24
        else:
            i, j = row >> 2, row & 3
            valid = (row < 12) & (j < 3)
        hit = (pixel == a + b * i + d * j) & valid
        parts[slot] = jnp.where(hit, 1.0, 0.0).astype(F32)
    order = sorted(range(10), key=lambda s: BASE[s])
    return jnp.concatenate([parts[s] for s in order], axis=0)


def place_matrix(me, n, so, cl):
    north, south = seam_steps(so, me, n)
    nz, sz = north == 0, south == 0

    def base(zero, slot_a, slot_b):
        return jnp.where(zero, jnp.int32(BASE[slot_a]), jnp.int32(BASE[slot_b]))

    def step(zero, slot_a, slot_b):
        return jnp.where(
            zero, jnp.int32(8 if ROWS[slot_a] == 32 else 4), jnp.int32(8 if ROWS[slot_b] == 32 else 4)
        )

    x = lax.broadcasted_iota(jnp.int32, (16, 256), 0)
    lane = lax.broadcasted_iota(jnp.int32, (16, 256), 1)
    live = [cl[me, c] == 1 for c in range(4)]

    def corner(c, i, j):
        zero, sa, sb = ((nz, 2, 3), (nz, 4, 5), (sz, 6, 7), (sz, 8, 9))[c]
        col = base(zero, sa, sb) + i * step(zero, sa, sb) + j
        return jnp.where(live[c], col, -1)

    blocks = []
    for y in range(14):
        if y < 3:
            left = corner(0, 2 - y, 2 - x)
            mid = base(nz, 3, 4) + (2 - y) * 8 + 10 - x
            right = corner(1, x - 11, 2 - y)
        elif y < 11:
            left = BASE[0] + (2 - x) * 8 + y - 3
            mid = jnp.full_like(x, -1)
            right = BASE[1] + (x - 11) * 8 + 10 - y
        else:
            left = corner(3, 2 - x, y - 11)
            mid = base(sz, 7, 8) + (y - 11) * 8 + x - 3
            right = corner(2, y - 11, x - 11)
        col = jnp.where(x < 3, left, jnp.where(x < 11, mid, jnp.where(x < 14, right, -1)))
        blocks.append(jnp.where(lane == col, 1.0, 0.0).astype(F32))
    blocks.append(jnp.zeros((32, 256), F32))
    return jnp.concatenate(blocks, axis=0)


def whole_wait(ref, sem):
    pltpu.make_async_copy(ref, ref, sem).wait()


def kernel(
    n,
    xin, cot, so, sf, cf, cl, dk, ng, ls, win_in, wout_in,
    dx_out, g_out, small_out,
    win, wout, pk, s_m, st_m, p_m, pt_m,
    pad, dpad, normed_s, inv_s, mixed_s, before_s, slope_s,
    u_s, h_s, dm_s, db_s, pa, pb,
    send_f, recv_f, send_b, recv_b,
    wsem, wsend, pksem, fs_sem, fr_sem, bs_sem, br_sem, psend, precv,
):
    seg = lax.axis_index("segment")
    me = lax.axis_index("tile")
    other = 1 - seg

    for l in range(2):
        b = 2 * seg + l
        pltpu.make_async_copy(win_in.at[l], win.at[b], wsem.at[0, b]).start()
        pltpu.make_async_copy(wout_in.at[l], wout.at[b], wsem.at[1, b]).start()

    barrier = pltpu.get_barrier_semaphore()
    for off in OFFSETS:
        pl.semaphore_signal(
            barrier, inc=1, device_id=(seg, lax.rem(me - off + n, n)), device_id_type=MESH
        )
    pl.semaphore_signal(barrier, inc=1, device_id=(other, me), device_id_type=MESH)

    for l in range(2):
        b = 2 * seg + l
        pk[b, 0:49, :] = dk[l].astype(F32)
        pk[b, 49:50, :] = ng[l : l + 1, :]
        pk[b, 50:51, :] = ls[l : l + 1, :]
        pk[b, 51:56, :] = jnp.zeros((5, C), F32)
    s_f = send_matrix(me, n, so, sf, cf)
    s_m[...] = s_f.astype(BF16)
    curb = xin[seg]
    send_f[0] = dot(s_m[...], curb).astype(BF16)

    pl.semaphore_wait(barrier, len(OFFSETS) + 1)

    def exchange(src, dst, ssem, rsem, sign):
        for slot in SEND_ORDER:
            rows = pl.ds(BASE[slot], ROWS[slot])
            pltpu.make_async_remote_copy(
                src_ref=src.at[rows],
                dst_ref=dst.at[rows],
                send_sem=ssem,
                recv_sem=rsem,
                device_id=(seg, lax.rem(me - sign * OFFSETS[slot] + n, n)),
                device_id_type=MESH,
            ).start()

    def to_partner(src, dst, ssem, rsem):
        return pltpu.make_async_remote_copy(
            src_ref=src, dst_ref=dst, send_sem=ssem, recv_sem=rsem,
            device_id=(other, me), device_id_type=MESH,
        )

    exchange(send_f.at[0], recv_f.at[0], fs_sem.at[0], fr_sem.at[0], 1)
    mine = pl.ds(2 * seg, 2)
    pk_copy = to_partner(pk.at[mine], pk.at[mine], pksem.at[0], pksem.at[1])
    pk_copy.start()
    w_copies = []
    for l in range(2):
        b = 2 * seg + l
        w_copies.append(to_partner(win_in.at[l], win.at[b], wsend.at[0, l], wsem.at[0, b]))
        w_copies.append(to_partner(wout_in.at[l], wout.at[b], wsend.at[1, l], wsem.at[1, b]))
    for copy in w_copies:
        copy.start()

    st_m[...] = jnp.transpose(s_f).astype(BF16)
    p_f = place_matrix(me, n, so, cl)
    p_m[...] = p_f.astype(BF16)
    pt_m[...] = jnp.transpose(p_f).astype(BF16)
    pk_copy.wait()

    def slope_of(b):
        before = before_s[...]
        slope_s[b] = (
            0.5 * (1.0 + lax.erf(before * ROOT_HALF))
            + before * jnp.exp(-0.5 * before * before) * INV_ROOT_TAU
        )

    for b in range(BLOCKS):
        if b > 0:
            send_f[b] = dot(s_m[...], curb).astype(BF16)
            exchange(send_f.at[b], recv_f.at[b], fs_sem.at[b], fr_sem.at[b], 1)
            slope_of(b - 1)
        cur = curb.astype(F32)
        whole_wait(recv_f.at[b], fr_sem.at[b])
        pad[b] = dot(p_m[...], recv_f[b]).reshape(16, 16, C)
        pad[b, 3:11, 3:11, :] = cur.reshape(8, 8, C)
        acc = jnp.zeros((8, 8, C), F32)
        for q in range(7):
            cols = pad[b, 0:14, q : q + 8, :]
            for r in range(7):
                acc = acc + cols[r : r + 8] * pk[b, 7 * r + q : 7 * r + q + 1, :]
        filtered = acc.reshape(64, C)
        centred = filtered - jnp.mean(filtered, axis=-1, keepdims=True)
        inv_std = lax.rsqrt(jnp.mean(centred * centred, axis=-1, keepdims=True) + EPSILON)
        normed = centred * inv_std
        normed_s[b] = normed
        inv_s[b] = jnp.broadcast_to(inv_std, (64, 128))
        unit = (normed * pk[b, 49:50, :]).astype(BF16)
        u_s[b] = unit
        whole_wait(win.at[b], wsem.at[0, b])
        before = dot(unit, win[b])
        before_s[...] = before
        hidden = (0.5 * before * (1.0 + lax.erf(before * ROOT_HALF))).astype(BF16)
        h_s[b] = hidden
        whole_wait(wout.at[b], wsem.at[1, b])
        mixed = dot(hidden, wout[b])
        mixed_s[b] = mixed
        curb = (cur + pk[b, 50:51, :] * mixed).astype(BF16)

        @pl.when(seg == 0)
        def _():
            to_partner(h_s.at[b], pb.at[b], psend.at[0, b], precv.at[1, b]).start()

        @pl.when(seg == 1)
        def _():
            to_partner(u_s.at[b], pa.at[b], psend.at[0, b], precv.at[0, b]).start()

    up = cot[seg].astype(F32)
    slope_of(BLOCKS - 1)
    for b in reversed(range(BLOCKS)):
        dm = (up * pk[b, 50:51, :]).astype(BF16)
        dm_s[b] = dm

        @pl.when(seg == 0)
        def _():
            to_partner(dm_s.at[b], pa.at[b], psend.at[1, b], precv.at[0, b]).start()

        d_hidden = dot(dm, wout[b], 1, 1)
        db = (d_hidden * slope_s[b]).astype(BF16)
        db_s[b] = db

        @pl.when(seg == 1)
        def _():
            to_partner(db_s.at[b], pb.at[b], psend.at[1, b], precv.at[1, b]).start()

        d_unit = dot(db, win[b], 1, 1)
        normed = normed_s[b]
        inv_std = inv_s[b, :, 0:1]
        dn = d_unit * pk[b, 49:50, :]
        df = inv_std * (
            dn
            - jnp.mean(dn, axis=-1, keepdims=True)
            - normed * jnp.mean(dn * normed, axis=-1, keepdims=True)
        )
        df = df.reshape(8, 8, C)
        dpad[...] = jnp.zeros((16, 16, C), F32)
        for q in range(7):
            rows = [None] * 14
            for r in range(7):
                term = df * pk[b, 7 * r + q : 7 * r + q + 1, :]
                for i in range(8):
                    part = term[i]
                    rows[r + i] = part if rows[r + i] is None else rows[r + i] + part
            dpad[0:14, q : q + 8, :] += jnp.stack(rows)
        send_b[b] = dot(pt_m[...], dpad[...].reshape(256, C).astype(BF16)).astype(BF16)
        exchange(send_b.at[b], recv_b.at[b], bs_sem.at[b], br_sem.at[b], -1)

        small_out[b, 49:50, :] = jnp.sum(d_unit * normed, axis=0, keepdims=True)
        small_out[b, 50:51, :] = jnp.sum(up * mixed_s[b], axis=0, keepdims=True)
        small_out[b, 51:56, :] = jnp.zeros((5, C), F32)
        for q in range(7):
            cols = pad[b, 0:14, q : q + 8, :]
            for r in range(7):
                tap = 7 * r + q
                prod = jnp.sum(df * cols[r : r + 8], axis=0)
                small_out[b, tap : tap + 1, :] = jnp.sum(prod, axis=0, keepdims=True)
        whole_wait(pa.at[b], precv.at[0, b])
        whole_wait(pb.at[b], precv.at[1, b])

        @pl.when(seg == 0)
        def _():
            g = dot(
                jnp.concatenate([u_s[b], pa[b]], axis=0),
                jnp.concatenate([db_s[b], pb[b]], axis=0), 0, 0,
            )
            for j in range(8):
                g_out[b, 256 * j : 256 * j + 256, :] = g[:, 128 * j : 128 * j + 128].astype(BF16)

        @pl.when(seg == 1)
        def _():
            g = dot(
                jnp.concatenate([h_s[b], pb[b]], axis=0),
                jnp.concatenate([dm_s[b], pa[b]], axis=0), 0, 0,
            )
            for j in range(2):
                g_out[b, 1024 * j : 1024 * j + 1024, :] = g[:, 128 * j : 128 * j + 128].astype(BF16)

        whole_wait(recv_b.at[b], br_sem.at[b])
        back = dot(st_m[...], recv_b[b])
        up = (up + dpad[3:11, 3:11, :].reshape(64, C) + back).astype(BF16)
        if b == 0:
            dx_out[...] = up
        up = up.astype(F32)

    for copy in w_copies:
        copy.wait_send()
    for b in range(BLOCKS):
        whole_wait(send_f.at[b], fs_sem.at[b])
        whole_wait(send_b.at[b], bs_sem.at[b])

        @pl.when(seg == 0)
        def _():
            whole_wait(h_s.at[b], psend.at[0, b])
            whole_wait(dm_s.at[b], psend.at[1, b])

        @pl.when(seg == 1)
        def _():
            whole_wait(u_s.at[b], psend.at[0, b])
            whole_wait(db_s.at[b], psend.at[1, b])


def local(
    inputs, cotangent, side_owner, side_from, corner_from, corner_live,
    depth_kernel, norm_gain, in_weight, out_weight, layer_scale,
):
    n = lax.axis_size("tile")
    factor = (2 * n * 64) ** (-0.5)
    vmem = pl.BlockSpec(memory_space=pltpu.VMEM)
    smem = pl.BlockSpec(memory_space=pltpu.SMEM)
    hbm = pl.BlockSpec(memory_space=pl.ANY)
    V = pltpu.VMEM
    dma = pltpu.SemaphoreType.DMA
    dx, g, small = pl.pallas_call(
        functools.partial(kernel, n),
        out_shape=(
            jax.ShapeDtypeStruct((64, C), BF16),
            jax.ShapeDtypeStruct((BLOCKS, 2048, 128), BF16),
            jax.ShapeDtypeStruct((BLOCKS, SMALL, C), F32),
        ),
        in_specs=[vmem, vmem, smem, smem, smem, smem, vmem, vmem, vmem, hbm, hbm],
        out_specs=(vmem, vmem, vmem),
        scratch_shapes=[
            V((BLOCKS, C, HID), BF16), V((BLOCKS, HID, C), BF16), V((BLOCKS, SMALL, C), F32),
            V((256, 64), BF16), V((64, 256), BF16), V((256, 256), BF16), V((256, 256), BF16),
            V((BLOCKS, 16, 16, C), F32), V((16, 16, C), F32),
            V((BLOCKS, 64, C), F32), V((BLOCKS, 64, 128), F32), V((BLOCKS, 64, C), F32),
            V((64, HID), F32), V((BLOCKS, 64, HID), F32),
            V((BLOCKS, 64, C), BF16), V((BLOCKS, 64, HID), BF16),
            V((BLOCKS, 64, C), BF16), V((BLOCKS, 64, HID), BF16),
            V((BLOCKS, 64, C), BF16), V((BLOCKS, 64, HID), BF16),
            V((BLOCKS, 256, C), BF16), V((BLOCKS, 256, C), BF16),
            V((BLOCKS, 256, C), BF16), V((BLOCKS, 256, C), BF16),
            dma((2, BLOCKS)), dma((2, 2)), dma((2,)),
            dma((BLOCKS,)), dma((BLOCKS,)), dma((BLOCKS,)), dma((BLOCKS,)),
            dma((2, BLOCKS)), dma((2, BLOCKS)),
        ],
        compiler_params=pltpu.CompilerParams(
            collective_id=0, has_side_effects=True, vmem_limit_bytes=40 * 1024 * 1024
        ),
    )(
        inputs.reshape(2, 64, C), cotangent.reshape(2, 64, C),
        side_owner, side_from, corner_from, corner_live,
        depth_kernel, norm_gain, layer_scale, in_weight, out_weight,
    )
    g = lax.psum(g, "tile")
    g = lax.all_to_all(g.reshape(2, 2, 2048, 128), "segment", 0, 0)
    g = g.astype(F32) * factor
    small = lax.psum(small, ("segment", "tile")) * factor
    small = lax.dynamic_slice_in_dim(small, 2 * lax.axis_index("segment"), 2, 0)
    d_in = g[0].reshape(2, 8, 256, 128).transpose(0, 2, 1, 3).reshape(2, C, HID)
    d_out = g[1].reshape(2, 2, 1024, 128).transpose(0, 2, 1, 3).reshape(2, HID, C)
    return dx.reshape(1, 8, 8, C), small[:, 0:49], small[:, 49], d_in, d_out, small[:, 50]


def solution(mesh):
    in_specs = (
        P(None, "tile", None, None), P(None, "tile", None, None),
        P(), P(), P(), P(),
        P("segment", None, None), P("segment", None), P("segment", None, None),
        P("segment", None, None), P("segment", None),
    )
    out_specs = (
        P("segment", "tile", None, None), P("segment", None, None), P("segment", None),
        P("segment", None, None), P("segment", None, None), P("segment", None),
    )
    return jax.shard_map(local, mesh=mesh, in_specs=in_specs, out_specs=out_specs, check_vma=False)
```

```python
import functools

import jax
import jax.numpy as jnp
from jax import lax
from jax.experimental import pallas as pl
from jax.experimental.pallas import tpu as pltpu
from jax.sharding import PartitionSpec as P

GW = 8
BLOCKS = 4
C = 256
HID = 1024
EPSILON = 1e-06
ROOT_HALF = 0.7071067811865476
INV_ROOT_TAU = 0.3989422804014327
MESH = pl.DeviceIdType.MESH
F32 = jnp.float32
BF16 = jnp.bfloat16

OFFSETS = (-1, 1, -GW - 1, -GW, -GW + 1, -GW + 2, GW + 1, GW, GW - 1, GW - 2)
ROWS = (32, 32, 16, 32, 32, 16, 16, 32, 32, 16)
BASE = (0, 32, 192, 64, 96, 208, 224, 128, 160, 240)
SEND_ORDER = (2, 5, 6, 9, 3, 4, 7, 8, 0, 1)
SMALL = 64
NX, NY, NZ = 4, 4, 8
VMEM_BYTES = 60 * 1024 * 1024


def dot(a, b, da=1, db=0):
    return lax.dot_general(a, b, (((da,), (db,)), ((), ())), preferred_element_type=F32)


def pick(code, values):
    out = jnp.int32(values[-1])
    for k in range(len(values) - 2, -1, -1):
        out = jnp.where(code == k, jnp.int32(values[k]), out)
    return out


def seam_steps(so, t, n):
    north = lax.rem(so[0, t] - t + GW + n, n)
    south = lax.rem(t + GW - so[2, t] + n, n)
    return north, south


def wanted_rim(slot, t, so, sf, cf, n):
    north, south = seam_steps(so, t, n)
    if slot == 0:
        return sf[3, t]
    if slot == 1:
        return sf[1, t]
    if slot == 2:
        return cf[0, t]
    if slot == 3:
        return jnp.where(north == 0, sf[0, t], cf[0, t])
    if slot == 4:
        return jnp.where(north == 1, sf[0, t], cf[1, t])
    if slot == 5:
        return cf[1, t]
    if slot == 6:
        return cf[2, t]
    if slot == 7:
        return jnp.where(south == 0, sf[2, t], cf[2, t])
    if slot == 8:
        return jnp.where(south == 1, sf[2, t], cf[3, t])
    return cf[3, t]


def send_matrix(me, n, so, sf, cf):
    parts = [None] * 10
    for slot in range(10):
        rows = ROWS[slot]
        code = wanted_rim(slot, lax.rem(me - OFFSETS[slot] + n, n), so, sf, cf, n)
        a = pick(code, (0, 7, 63, 56))
        b = pick(code, (8, -1, -8, 1))
        d = pick(code, (1, 8, -1, -8))
        row = lax.broadcasted_iota(jnp.int32, (rows, 64), 0)
        pixel = lax.broadcasted_iota(jnp.int32, (rows, 64), 1)
        if rows == 32:
            i, j = row >> 3, row & 7
            valid = row < 24
        else:
            i, j = row >> 2, row & 3
            valid = (row < 12) & (j < 3)
        hit = (pixel == a + b * i + d * j) & valid
        parts[slot] = jnp.where(hit, 1.0, 0.0).astype(F32)
    order = sorted(range(10), key=lambda s: BASE[s])
    return jnp.concatenate([parts[s] for s in order], axis=0)


def place_matrix(me, n, so, cl):
    north, south = seam_steps(so, me, n)
    nz, sz = north == 0, south == 0

    def base(zero, slot_a, slot_b):
        return jnp.where(zero, jnp.int32(BASE[slot_a]), jnp.int32(BASE[slot_b]))

    def step(zero, slot_a, slot_b):
        return jnp.where(
            zero, jnp.int32(8 if ROWS[slot_a] == 32 else 4), jnp.int32(8 if ROWS[slot_b] == 32 else 4)
        )

    x = lax.broadcasted_iota(jnp.int32, (16, 256), 0)
    lane = lax.broadcasted_iota(jnp.int32, (16, 256), 1)
    live = [cl[c, me] == 1 for c in range(4)]

    def corner(c, i, j):
        zero, sa, sb = ((nz, 2, 3), (nz, 4, 5), (sz, 6, 7), (sz, 8, 9))[c]
        col = base(zero, sa, sb) + i * step(zero, sa, sb) + j
        return jnp.where(live[c], col, -1)

    blocks = []
    for y in range(14):
        if y < 3:
            left = corner(0, 2 - y, 2 - x)
            mid = base(nz, 3, 4) + (2 - y) * 8 + 10 - x
            right = corner(1, x - 11, 2 - y)
        elif y < 11:
            left = BASE[0] + (2 - x) * 8 + y - 3
            mid = jnp.full_like(x, -1)
            right = BASE[1] + (x - 11) * 8 + 10 - y
        else:
            left = corner(3, 2 - x, y - 11)
            mid = base(sz, 7, 8) + (y - 11) * 8 + x - 3
            right = corner(2, y - 11, x - 11)
        col = jnp.where(x < 3, left, jnp.where(x < 11, mid, jnp.where(x < 14, right, -1)))
        blocks.append(jnp.where(lane == col, 1.0, 0.0).astype(F32))
    blocks.append(jnp.zeros((32, 256), F32))
    return jnp.concatenate(blocks, axis=0)


def whole_wait(ref, sem):
    pltpu.make_async_copy(ref, ref, sem).wait()


def kernel(
    n,
    xin, cot, so_in, sf_in, cf_in, cl_in, dk_in, ng_in, ls_in, win_in, wout_in,
    dx_out, gin_out, gout_out, small_s,
    g_s, r1, g2, r2, g3, r3, ag, sm, sr0, s0, sr1, s1, sr2, s2, sr3, s3,
    so, sf, cf, cl, x_s, x0_s, cot_s, s0_m, dk_s, ng_s, ls_s,
    win, wout, pk, s_m, st_m, p_m, pt_m,
    pad, dpad, normed_s, inv_s, mixed_s, before_s, slope_s,
    u_s, h_s, dm_s, db_s, pa, pb,
    send_f, recv_f, send_b, recv_b,
    wsem, wsend, pksem, fs_sem, fr_sem, bs_sem, br_sem, psend, precv,
    ms_sem, mr_sem, go_sem, ss_sem, sr_sem, so_sem, in_sem, xr_sem,
):
    seg = lax.axis_index("segment")
    me = lax.axis_index("tile")
    other = 1 - seg

    seams = [
        pltpu.make_async_copy(src, dst, in_sem.at[k])
        for k, (src, dst) in enumerate(((so_in, so), (sf_in, sf), (cf_in, cf), (cl_in, cl)))
    ]
    x_copy = pltpu.make_async_copy(xin.at[seg], x_s, in_sem.at[4])
    small_in = [
        pltpu.make_async_copy(src, dst, in_sem.at[5 + k])
        for k, (src, dst) in enumerate(((dk_in, dk_s), (ng_in, ng_s), (ls_in, ls_s)))
    ]
    for copy in [*seams, x_copy, *small_in]:
        copy.start()

    z = lax.rem(me, NZ)
    y = lax.rem(me // NZ, NY)
    x = me // (NZ * NY)
    at1, at2 = x + seg * (y - x), y + seg * (x - y)
    stride1 = NY * NZ - seg * (NY * NZ - NZ)
    stride2 = NZ + seg * (NY * NZ - NZ)

    def device_of(t):
        row = t // NZ
        hi = row // NY
        lo = row - hi * NY
        lo = lo + lax.rem(hi, 2) * (NY - 1 - 2 * lo)
        return (hi * NY + lo) * NZ + lax.rem(t, NZ)

    odd = lax.rem(x, 2)
    tile = device_of(me)
    mirror = tile

    def peer1(d):
        to = lax.rem(at1 + d, NX)
        return to, me + (to - at1) * stride1

    def peer2(d):
        to = lax.rem(at2 + d, NX)
        return to, me + (to - at2) * stride2

    def peer3(d):
        to = lax.rem(z + d, NZ)
        return to, me + to - z

    barrier = pltpu.get_barrier_semaphore()
    partners = [(seg, peer1(d)[1]) for d in range(1, NX)]
    partners += [(other, peer1(d)[1]) for d in range(1, NX)]
    partners += [(seg, peer2(d)[1]) for d in range(1, NX)]
    partners += [(other, peer2(d)[1]) for d in range(1, NX)]
    partners += [(seg, peer3(d)[1]) for d in range(1, NZ)]
    for off in OFFSETS:
        if abs(off) != GW:
            partners.append((seg, lax.rem(tile + off + n, n)))
        partners.append((seg, device_of(lax.rem(tile + off + n, n))))
    partners.append((other, me))
    for partner in partners:
        pl.semaphore_signal(barrier, inc=1, device_id=partner, device_id_type=MESH)

    @pl.when(odd == 1)
    def _():
        pl.semaphore_signal(barrier, inc=1, device_id=(seg, mirror), device_id_type=MESH)

    stays = {off: tile == lax.rem(me - off + n, n) for off in (-GW, GW)}
    signals = len(partners) + odd
    for off, stay in stays.items():
        signals = signals + jnp.where(stay, 0, 1)

        @pl.when(jnp.logical_not(stay))
        def _():
            pl.semaphore_signal(
                barrier, inc=1, device_id=(seg, lax.rem(tile + off + n, n)), device_id_type=MESH
            )

    mine = pl.ds(2 * seg, 2)
    for l in range(2):
        b = 2 * seg + l
        pltpu.make_async_copy(win_in.at[l], win.at[b], wsem.at[0, b]).start()
        pltpu.make_async_copy(wout_in.at[l], wout.at[b], wsem.at[1, b]).start()

    for copy in seams:
        copy.wait()
    s0_m[...] = send_matrix(me, n, so, sf, cf).astype(BF16)
    x_copy.wait()
    send_f[0] = dot(s0_m[...], x_s[...]).astype(BF16)

    for copy in small_in:
        copy.wait()
    taps = dk_s[...].astype(F32)
    for l in range(2):
        b = 2 * seg + l
        pk[b, 0:49, :] = taps[:, l, :]
        pk[b, 49:50, :] = ng_s[l : l + 1, :]
        pk[b, 50:51, :] = ls_s[l : l + 1, :]
        pk[b, 51:64, :] = jnp.zeros((13, C), F32)

    pl.semaphore_wait(barrier, signals)

    def exchange(src, dst, ssem, rsem, sign, home):
        for slot in SEND_ORDER:
            off = OFFSETS[slot]
            rows = pl.ds(BASE[slot], ROWS[slot])

            def go():
                pltpu.make_async_remote_copy(
                    src_ref=src.at[rows],
                    dst_ref=dst.at[rows],
                    send_sem=ssem,
                    recv_sem=rsem,
                    device_id=(seg, device_of(lax.rem(home - sign * off + n, n))),
                    device_id_type=MESH,
                ).start()

            if home is tile or off not in stays:
                go()
            else:
                pl.when(jnp.logical_not(stays[off]))(go)

                @pl.when(stays[off])
                def _():
                    pltpu.make_async_copy(src.at[rows], dst.at[rows], rsem).start()

    def to_partner(src, dst, ssem, rsem):
        return pltpu.make_async_remote_copy(
            src_ref=src, dst_ref=dst, send_sem=ssem, recv_sem=rsem,
            device_id=(other, me), device_id_type=MESH,
        )

    exchange(send_f.at[0], recv_f.at[0], fs_sem.at[0], fr_sem.at[0], 1, me)

    @pl.when(odd == 1)
    def _():
        for k, (src, dst) in enumerate(((xin, x0_s), (cot, cot_s))):
            pltpu.make_async_remote_copy(
                src_ref=src.at[seg], dst_ref=dst, send_sem=xr_sem.at[0, k], recv_sem=xr_sem.at[1, k],
                device_id=(seg, mirror), device_id_type=MESH,
            ).start()

    @pl.when(odd == 0)
    def _():
        for k, (src, dst) in enumerate(((xin, x0_s), (cot, cot_s))):
            pltpu.make_async_copy(src.at[seg], dst, xr_sem.at[1, k]).start()

    pk_copy = to_partner(pk.at[mine], pk.at[mine], pksem.at[0], pksem.at[1])
    pk_copy.start()
    w_copies = []
    for l in range(2):
        b = 2 * seg + l
        w_copies.append(to_partner(win_in.at[l], win.at[b], wsend.at[0, l], wsem.at[0, b]))
        w_copies.append(to_partner(wout_in.at[l], wout.at[b], wsend.at[1, l], wsem.at[1, b]))
    for copy in w_copies:
        copy.start()

    s_f = send_matrix(tile, n, so, sf, cf)
    s_m[...] = s_f.astype(BF16)
    st_m[...] = jnp.transpose(s_f).astype(BF16)
    p_f = place_matrix(tile, n, so, cl)
    p_m[...] = p_f.astype(BF16)
    pt_m[...] = jnp.transpose(p_f).astype(BF16)
    pk_copy.wait()
    whole_wait(x0_s, xr_sem.at[1, 0])
    curb = x0_s[...]

    q1, q2, q3 = 2048 // NX, 2048 // NX // NX, 2048 // NX // NX // NZ
    w1 = 64 // NX

    def send(src, dst, ssem, rsem, device):
        pltpu.make_async_remote_copy(
            src_ref=src, dst_ref=dst, send_sem=ssem, recv_sem=rsem,
            device_id=device, device_id_type=MESH,
        ).start()

    def main_chain(b):
        l, owner = b % 2, b // 2
        for d in range(1, NX):
            to, t = peer1(d)
            send(g_s.at[b, pl.ds(to * q1, q1)], r1.at[b, d - 1], ms_sem.at[0, b], mr_sem.at[0, b], (seg, t))
        yield
        whole_wait(r1.at[b], mr_sem.at[0, b])
        total = g_s[b, pl.ds(at1 * q1, q1), :].astype(F32)
        for d in range(NX - 1):
            total = total + r1[b, d].astype(F32)
        g2[b] = total.astype(BF16)
        for d in range(1, NX):
            to, t = peer2(d)
            send(g2.at[b, pl.ds(to * q2, q2)], r2.at[b, d - 1], ms_sem.at[1, b], mr_sem.at[1, b], (seg, t))
        yield
        whole_wait(r2.at[b], mr_sem.at[1, b])
        total = g2[b, pl.ds(at2 * q2, q2), :].astype(F32)
        for d in range(NX - 1):
            total = total + r2[b, d].astype(F32)
        g3[b] = total.astype(BF16)
        for d in range(1, NZ):
            to, t = peer3(d)
            send(g3.at[b, pl.ds(to * q3, q3)], r3.at[b, d - 1], ms_sem.at[2, b], mr_sem.at[2, b], (seg, t))
        yield
        whole_wait(r3.at[b], mr_sem.at[2, b])
        total = g3[b, pl.ds(z * q3, q3), :].astype(F32)
        for d in range(NZ - 1):
            total = total + r3[b, d].astype(F32)
        here = pl.ds(at2 * q2 + z * q3, q3)
        ag[b, here, :] = total.astype(BF16)
        for d in range(1, NZ):
            send(ag.at[b, here], ag.at[b, here], ms_sem.at[3, b], mr_sem.at[3, b], (seg, peer3(d)[1]))
        yield
        whole_wait(ag.at[b, pl.ds(0, (NZ - 1) * q3)], mr_sem.at[3, b])
        here2 = pl.ds(at2 * q2, q2)
        for d in range(1, NX):
            send(ag.at[b, here2], ag.at[b, here2], ms_sem.at[4, b], mr_sem.at[4, b], (seg, peer2(d)[1]))
        yield
        whole_wait(ag.at[b, pl.ds(0, (NX - 1) * q2)], mr_sem.at[4, b])
        for kind in range(2):

            @pl.when(seg == kind)
            def _():
                if kind == 0:
                    first = pl.multiple_of(at1 * (q1 // 2), 128)
                    pairs = [
                        (ag.at[b, pl.ds(256 * j, 256)], gin_out.at[l, :, pl.ds(first + 128 * j, 128)])
                        for j in range(q1 // 256)
                    ]
                else:
                    rows = pl.multiple_of(lax.rem(at1 * q1, 1024), 16)
                    column = pl.multiple_of((at1 * q1 // 1024) * 128, 128)
                    pairs = [(ag.at[b], gout_out.at[l, pl.ds(rows, q1), pl.ds(column, 128)])]
                for d in range(1, NX):
                    for src, dst in pairs:
                        send(src, dst, ms_sem.at[5, b], go_sem.at[l, kind], (owner, peer1(d)[1]))
                for src, dst in pairs:
                    if kind == owner:
                        pltpu.make_async_copy(src, dst, go_sem.at[l, kind]).start()
                    else:
                        send(src, dst, ms_sem.at[6, b], go_sem.at[l, kind], (other, me))

    def small_chain(b):
        l, owner = b % 2, b // 2
        send(sm.at[b, pl.ds(other * 64, 64)], sr0.at[b], ss_sem.at[0, b], sr_sem.at[0, b], (other, me))
        yield
        whole_wait(sr0.at[b], sr_sem.at[0, b])
        s0[b] = sm[b, pl.ds(seg * 64, 64), :] + sr0[b]
        for d in range(1, NX):
            to, t = peer1(d)
            send(s0.at[b, pl.ds(to * w1, w1)], sr1.at[b, d - 1], ss_sem.at[1, b], sr_sem.at[1, b], (seg, t))
        yield
        whole_wait(sr1.at[b], sr_sem.at[1, b])
        s1[b] = s0[b, pl.ds(at1 * w1, w1), :] + jnp.sum(sr1[b], axis=0)
        for d in range(1, NX):
            send(s1.at[b], sr2.at[b, d - 1], ss_sem.at[2, b], sr_sem.at[2, b], (seg, peer2(d)[1]))
        yield
        whole_wait(sr2.at[b], sr_sem.at[2, b])
        s2[b] = s1[b] + jnp.sum(sr2[b], axis=0)
        for d in range(1, NZ):
            send(s2.at[b], sr3.at[b, d - 1], ss_sem.at[3, b], sr_sem.at[3, b], (seg, peer3(d)[1]))
        yield
        whole_wait(sr3.at[b], sr_sem.at[3, b])
        s3[b] = s2[b] + jnp.sum(sr3[b], axis=0)
        out = small_s.at[l, pl.ds(seg * 64 + at1 * w1, w1)]
        for d in range(1, NX):
            send(s3.at[b], out, ss_sem.at[4, b], so_sem.at[l], (owner, peer1(d)[1]))

        @pl.when(seg == owner)
        def _():
            pltpu.make_async_copy(s3.at[b], out, so_sem.at[l]).start()

        @pl.when(seg != owner)
        def _():
            send(s3.at[b], out, ss_sem.at[5, b], so_sem.at[l], (other, me))

    chains = []

    def begin(chain):
        next(chain)
        chains.append(chain)

    def advance(which=None):
        for chain in list(chains if which is None else which):
            if chain in chains and next(chain, True):
                chains.remove(chain)

    def slope_of(b):
        before = before_s[...]
        slope_s[b] = (
            0.5 * (1.0 + lax.erf(before * ROOT_HALF))
            + before * jnp.exp(-0.5 * before * before) * INV_ROOT_TAU
        )

    for b in range(BLOCKS):
        if b > 0:
            send_f[b] = dot(s_m[...], curb).astype(BF16)
            exchange(send_f.at[b], recv_f.at[b], fs_sem.at[b], fr_sem.at[b], 1, tile)
            slope_of(b - 1)
        cur = curb.astype(F32)
        whole_wait(recv_f.at[b], fr_sem.at[b])
        pad[b] = dot(p_m[...], recv_f[b]).reshape(16, 16, C)
        pad[b, 3:11, 3:11, :] = cur.reshape(8, 8, C)
        acc = jnp.zeros((8, 8, C), F32)
        for q in range(7):
            cols = pad[b, 0:14, q : q + 8, :]
            for r in range(7):
                acc = acc + cols[r : r + 8] * pk[b, 7 * r + q : 7 * r + q + 1, :]
        filtered = acc.reshape(64, C)
        centred = filtered - jnp.mean(filtered, axis=-1, keepdims=True)
        inv_std = lax.rsqrt(jnp.mean(centred * centred, axis=-1, keepdims=True) + EPSILON)
        normed = centred * inv_std
        normed_s[b] = normed
        inv_s[b] = jnp.broadcast_to(inv_std, (64, 128))
        unit = (normed * pk[b, 49:50, :]).astype(BF16)
        u_s[b] = unit
        whole_wait(win.at[b], wsem.at[0, b])
        before = dot(unit, win[b])
        before_s[...] = before
        hidden = (0.5 * before * (1.0 + lax.erf(before * ROOT_HALF))).astype(BF16)
        h_s[b] = hidden
        whole_wait(wout.at[b], wsem.at[1, b])
        mixed = dot(hidden, wout[b])
        mixed_s[b] = mixed
        curb = (cur + pk[b, 50:51, :] * mixed).astype(BF16)

        @pl.when(seg == 0)
        def _():
            to_partner(h_s.at[b], pb.at[b], psend.at[0, b], precv.at[1, b]).start()

        @pl.when(seg == 1)
        def _():
            to_partner(u_s.at[b], pa.at[b], psend.at[0, b], precv.at[0, b]).start()

    whole_wait(cot_s, xr_sem.at[1, 1])
    up = cot_s[...].astype(F32)
    slope_of(BLOCKS - 1)
    for b in reversed(range(BLOCKS)):
        dm = (up * pk[b, 50:51, :]).astype(BF16)
        dm_s[b] = dm

        @pl.when(seg == 0)
        def _():
            to_partner(dm_s.at[b], pa.at[b], psend.at[1, b], precv.at[0, b]).start()

        d_hidden = dot(dm, wout[b], 1, 1)
        db = (d_hidden * slope_s[b]).astype(BF16)
        db_s[b] = db

        @pl.when(seg == 1)
        def _():
            to_partner(db_s.at[b], pb.at[b], psend.at[1, b], precv.at[1, b]).start()

        d_unit = dot(db, win[b], 1, 1)
        normed = normed_s[b]
        inv_std = inv_s[b, :, 0:1]
        dn = d_unit * pk[b, 49:50, :]
        df = inv_std * (
            dn
            - jnp.mean(dn, axis=-1, keepdims=True)
            - normed * jnp.mean(dn * normed, axis=-1, keepdims=True)
        )
        df = df.reshape(8, 8, C)
        older = list(chains)

        def put(row, value):
            sm[b, row : row + 1, :] = value[:, 0:128]
            sm[b, 64 + row : 65 + row, :] = value[:, 128:256]

        def small_grads():
            put(49, jnp.sum(d_unit * normed, axis=0, keepdims=True))
            put(50, jnp.sum(up * mixed_s[b], axis=0, keepdims=True))
            sm[b, 51:64, :] = jnp.zeros((13, 128), F32)
            sm[b, 115:128, :] = jnp.zeros((13, 128), F32)
            for q in range(7):
                cols = pad[b, 0:14, q : q + 8, :]
                for r in range(7):
                    tap = 7 * r + q
                    prod = jnp.sum(df * cols[r : r + 8], axis=0)
                    put(tap, jnp.sum(prod, axis=0, keepdims=True))
            begin(small_chain(b))

        def weight_grads():
            whole_wait(pa.at[b], precv.at[0, b])
            whole_wait(pb.at[b], precv.at[1, b])

            @pl.when(seg == 0)
            def _():
                g = dot(
                    jnp.concatenate([u_s[b], pa[b]], axis=0),
                    jnp.concatenate([db_s[b], pb[b]], axis=0), 0, 0,
                )
                for j in range(8):
                    g_s[b, 256 * j : 256 * j + 256, :] = g[:, 128 * j : 128 * j + 128].astype(BF16)

            @pl.when(seg == 1)
            def _():
                g = dot(
                    jnp.concatenate([h_s[b], pb[b]], axis=0),
                    jnp.concatenate([dm_s[b], pa[b]], axis=0), 0, 0,
                )
                for j in range(2):
                    g_s[b, 1024 * j : 1024 * j + 1024, :] = g[:, 128 * j : 128 * j + 128].astype(BF16)

            begin(main_chain(b))

        if b == 0:
            weight_grads()
            small_grads()
        advance(older)
        dpad[...] = jnp.zeros((16, 16, C), F32)
        for q in range(7):
            rows = [None] * 14
            for r in range(7):
                term = df * pk[b, 7 * r + q : 7 * r + q + 1, :]
                for i in range(8):
                    part = term[i]
                    rows[r + i] = part if rows[r + i] is None else rows[r + i] + part
            dpad[0:14, q : q + 8, :] += jnp.stack(rows)
        send_b[b] = dot(pt_m[...], dpad[...].reshape(256, C).astype(BF16)).astype(BF16)
        exchange(send_b.at[b], recv_b.at[b], bs_sem.at[b], br_sem.at[b], -1, tile)

        advance(older)
        if b > 0:
            small_grads()
            weight_grads()
        whole_wait(recv_b.at[b], br_sem.at[b])
        back = dot(st_m[...], recv_b[b])
        up = (up + dpad[3:11, 3:11, :].reshape(64, C) + back).astype(BF16)
        if b == 0:
            x_s[...] = up

            @pl.when(odd == 1)
            def _():
                pltpu.make_async_remote_copy(
                    src_ref=x_s, dst_ref=dx_out, send_sem=xr_sem.at[0, 2], recv_sem=xr_sem.at[1, 2],
                    device_id=(seg, mirror), device_id_type=MESH,
                ).start()

            @pl.when(odd == 0)
            def _():
                pltpu.make_async_copy(x_s, dx_out, xr_sem.at[1, 2]).start()

        up = up.astype(F32)

    while chains:
        advance()
    for l in range(2):
        whole_wait(small_s.at[l], so_sem.at[l])
        whole_wait(gin_out.at[l], go_sem.at[l, 0])
        whole_wait(gout_out.at[l], go_sem.at[l, 1])
    whole_wait(dx_out, xr_sem.at[1, 2])
    stay = jnp.logical_or(stays[-GW], stays[GW])

    @pl.when(stay)
    def _():
        whole_wait(send_f.at[0, pl.ds(0, 224)], fs_sem.at[0])

    @pl.when(jnp.logical_not(stay))
    def _():
        whole_wait(send_f.at[0], fs_sem.at[0])

    @pl.when(odd == 1)
    def _():
        for k in range(3):
            whole_wait(x_s, xr_sem.at[0, k])

    for copy in w_copies:
        copy.wait_send()
    for b in range(BLOCKS):
        if b > 0:
            whole_wait(send_f.at[b], fs_sem.at[b])
        whole_wait(send_b.at[b], bs_sem.at[b])
        whole_wait(r1.at[b], ms_sem.at[0, b])
        whole_wait(r2.at[b], ms_sem.at[1, b])
        whole_wait(r3.at[b], ms_sem.at[2, b])
        whole_wait(r3.at[b], ms_sem.at[3, b])
        whole_wait(r2.at[b], ms_sem.at[4, b])
        whole_wait(r1.at[b], ms_sem.at[5, b])
        whole_wait(sr0.at[b], ss_sem.at[0, b])
        whole_wait(sr1.at[b], ss_sem.at[1, b])
        whole_wait(sr2.at[b], ss_sem.at[2, b])
        whole_wait(sr3.at[b], ss_sem.at[3, b])
        whole_wait(sr1.at[b], ss_sem.at[4, b])

        @pl.when(seg != b // 2)
        def _():
            whole_wait(ag.at[b], ms_sem.at[6, b])
            whole_wait(s3.at[b], ss_sem.at[5, b])

        @pl.when(seg == 0)
        def _():
            whole_wait(h_s.at[b], psend.at[0, b])
            whole_wait(dm_s.at[b], psend.at[1, b])

        @pl.when(seg == 1)
        def _():
            whole_wait(u_s.at[b], psend.at[0, b])
            whole_wait(db_s.at[b], psend.at[1, b])


def finish(factor, dx, gin, gout, small, dx_out, gin_out, gout_out, gk_out, gg_out, gs_out):
    gin_out[...] = gin[...].astype(F32) * factor
    gout_out[...] = gout[...].astype(F32) * factor
    dx_out[...] = dx[...].reshape(dx_out.shape)
    for l in range(2):
        total = jnp.concatenate([small[l, 0:64, :], small[l, 64:128, :]], axis=1) * factor
        gk_out[:, l, :] = total[0:49]
        gg_out[l : l + 1, :] = total[49:50]
        gs_out[l : l + 1, :] = total[50:51]


def local(
    inputs, cotangent, side_owner, side_from, corner_from, corner_live,
    depth_kernel, norm_gain, in_weight, out_weight, layer_scale,
):
    n = lax.axis_size("tile")
    factor = (2 * n * 64) ** (-0.5)
    vmem = pl.BlockSpec(memory_space=pltpu.VMEM)
    hbm = pl.BlockSpec(memory_space=pl.ANY)
    V = pltpu.VMEM
    S = pltpu.SMEM
    shape = jax.ShapeDtypeStruct
    q1, q2, q3 = 2048 // NX, 2048 // NX // NX, 2048 // NX // NX // NZ
    w1 = 64 // NX
    dma = pltpu.SemaphoreType.DMA
    dx, d_in, d_out, small = pl.pallas_call(
        functools.partial(kernel, n),
        out_shape=(
            shape((64, C), BF16), shape((2, C, HID), BF16), shape((2, HID, C), BF16), shape((2, 128, 128), F32),
        ),
        in_specs=[hbm] * 11,
        out_specs=(hbm,) * 4,
        scratch_shapes=[
            V((BLOCKS, 2048, 128), BF16), V((BLOCKS, NX - 1, q1, 128), BF16), V((BLOCKS, q1, 128), BF16),
            V((BLOCKS, NX - 1, q2, 128), BF16), V((BLOCKS, q2, 128), BF16), V((BLOCKS, NZ - 1, q3, 128), BF16),
            V((BLOCKS, q1, 128), BF16), V((BLOCKS, 128, 128), F32),
            V((BLOCKS, 64, 128), F32), V((BLOCKS, 64, 128), F32),
            V((BLOCKS, NX - 1, w1, 128), F32), V((BLOCKS, w1, 128), F32),
            V((BLOCKS, NX - 1, w1, 128), F32), V((BLOCKS, w1, 128), F32),
            V((BLOCKS, NZ - 1, w1, 128), F32), V((BLOCKS, w1, 128), F32),
            S((4, n), jnp.int32), S((4, n), jnp.int32), S((4, n), jnp.int32), S((4, n), jnp.int32),
            V((64, C), BF16), V((64, C), BF16), V((64, C), BF16), V((256, 64), BF16),
            V((49, 2, C), BF16), V((2, C), F32), V((2, C), F32),
            V((BLOCKS, C, HID), BF16), V((BLOCKS, HID, C), BF16), V((BLOCKS, SMALL, C), F32),
            V((256, 64), BF16), V((64, 256), BF16), V((256, 256), BF16), V((256, 256), BF16),
            V((BLOCKS, 16, 16, C), F32), V((16, 16, C), F32),
            V((BLOCKS, 64, C), F32), V((BLOCKS, 64, 128), F32), V((BLOCKS, 64, C), F32),
            V((64, HID), F32), V((BLOCKS, 64, HID), F32),
            V((BLOCKS, 64, C), BF16), V((BLOCKS, 64, HID), BF16),
            V((BLOCKS, 64, C), BF16), V((BLOCKS, 64, HID), BF16),
            V((BLOCKS, 64, C), BF16), V((BLOCKS, 64, HID), BF16),
            V((BLOCKS, 256, C), BF16), V((BLOCKS, 256, C), BF16),
            V((BLOCKS, 256, C), BF16), V((BLOCKS, 256, C), BF16),
            dma((2, BLOCKS)), dma((2, 2)), dma((2,)),
            dma((BLOCKS,)), dma((BLOCKS,)), dma((BLOCKS,)), dma((BLOCKS,)),
            dma((2, BLOCKS)), dma((2, BLOCKS)),
            dma((7, BLOCKS)), dma((5, BLOCKS)), dma((2, 2)), dma((6, BLOCKS)), dma((4, BLOCKS)), dma((2,)),
            dma((8,)), dma((2, 3)),
        ],
        compiler_params=pltpu.CompilerParams(
            collective_id=0, has_side_effects=True, vmem_limit_bytes=VMEM_BYTES
        ),
    )(
        inputs.reshape(2, 64, C), cotangent.reshape(2, 64, C),
        side_owner.T, side_from.T, corner_from.T, corner_live.T,
        depth_kernel.transpose(1, 0, 2), norm_gain, layer_scale, in_weight, out_weight,
    )
    dx, d_in, d_out, d_kernel, d_gain, d_scale = pl.pallas_call(
        functools.partial(finish, factor),
        grid=(4,),
        out_shape=(
            shape((1, 8, 8, C), BF16), shape((2, C, HID), F32), shape((2, HID, C), F32),
            shape((49, 2, C), F32), shape((2, C), F32), shape((2, C), F32),
        ),
        in_specs=[
            pl.BlockSpec((64, C), lambda i: (0, 0)),
            pl.BlockSpec((2, C // 4, HID), lambda i: (0, i, 0)),
            pl.BlockSpec((2, HID // 4, C), lambda i: (0, i, 0)),
            pl.BlockSpec((2, 128, 128), lambda i: (0, 0, 0)),
        ],
        out_specs=(
            pl.BlockSpec((1, 8, 8, C), lambda i: (0, 0, 0, 0)),
            pl.BlockSpec((2, C // 4, HID), lambda i: (0, i, 0)),
            pl.BlockSpec((2, HID // 4, C), lambda i: (0, i, 0)),
            pl.BlockSpec((49, 2, C), lambda i: (0, 0, 0)),
            pl.BlockSpec((2, C), lambda i: (0, 0)),
            pl.BlockSpec((2, C), lambda i: (0, 0)),
        ),
        compiler_params=pltpu.CompilerParams(vmem_limit_bytes=VMEM_BYTES),
    )(dx, d_in, d_out, small)
    return dx, d_kernel.transpose(1, 0, 2), d_gain, d_in, d_out, d_scale


def solution(mesh):
    in_specs = (
        P(None, "tile", None, None), P(None, "tile", None, None),
        P(), P(), P(), P(),
        P("segment", None, None), P("segment", None), P("segment", None, None),
        P("segment", None, None), P("segment", None),
    )
    out_specs = (
        P("segment", "tile", None, None), P("segment", None, None), P("segment", None),
        P("segment", None, None), P("segment", None, None), P("segment", None),
    )
    return jax.shard_map(local, mesh=mesh, in_specs=in_specs, out_specs=out_specs, check_vma=False)
```

```python
import functools

import jax
import jax.numpy as jnp
from jax import lax
from jax.experimental import pallas as pl
from jax.experimental.pallas import tpu as pltpu
from jax.sharding import PartitionSpec as P

GW = 8
BLOCKS = 4
C = 256
HID = 1024
EPSILON = 1e-06
ROOT_HALF = 0.7071067811865476
INV_ROOT_TAU = 0.3989422804014327
MESH = pl.DeviceIdType.MESH
F32 = jnp.float32
BF16 = jnp.bfloat16

OFFSETS = (-1, 1, -GW - 1, -GW, -GW + 1, -GW + 2, GW + 1, GW, GW - 1, GW - 2)
ROWS = (32, 32, 16, 32, 32, 16, 16, 32, 32, 16)
BASE = (0, 32, 192, 64, 96, 208, 224, 128, 160, 240)
SEND_ORDER = (2, 5, 6, 9, 3, 4, 7, 8, 0, 1)
SMALL = 64
NX, NY, NZ = 4, 4, 8
VMEM_BYTES = 60 * 1024 * 1024
SHORT = ()


def dot(a, b, da=1, db=0):
    return lax.dot_general(a, b, (((da,), (db,)), ((), ())), preferred_element_type=F32)


def pick(code, values):
    out = jnp.int32(values[-1])
    for k in range(len(values) - 2, -1, -1):
        out = jnp.where(code == k, jnp.int32(values[k]), out)
    return out


def seam_steps(so, t, n):
    north = lax.rem(so[0, t] - t + GW + n, n)
    south = lax.rem(t + GW - so[2, t] + n, n)
    return north, south


def wanted_rim(slot, t, so, sf, cf, n):
    north, south = seam_steps(so, t, n)
    if slot == 0:
        return sf[3, t]
    if slot == 1:
        return sf[1, t]
    if slot == 2:
        return cf[0, t]
    if slot == 3:
        return jnp.where(north == 0, sf[0, t], cf[0, t])
    if slot == 4:
        return jnp.where(north == 1, sf[0, t], cf[1, t])
    if slot == 5:
        return cf[1, t]
    if slot == 6:
        return cf[2, t]
    if slot == 7:
        return jnp.where(south == 0, sf[2, t], cf[2, t])
    if slot == 8:
        return jnp.where(south == 1, sf[2, t], cf[3, t])
    return cf[3, t]


def send_matrix(me, n, so, sf, cf):
    parts = [None] * 10
    for slot in range(10):
        rows = ROWS[slot]
        code = wanted_rim(slot, lax.rem(me - OFFSETS[slot] + n, n), so, sf, cf, n)
        a = pick(code, (0, 7, 63, 56))
        b = pick(code, (8, -1, -8, 1))
        d = pick(code, (1, 8, -1, -8))
        row = lax.broadcasted_iota(jnp.int32, (rows, 64), 0)
        pixel = lax.broadcasted_iota(jnp.int32, (rows, 64), 1)
        if rows == 32:
            i, j = row >> 3, row & 7
            valid = row < 24
        else:
            i, j = row >> 2, row & 3
            valid = (row < 12) & (j < 3)
        hit = (pixel == a + b * i + d * j) & valid
        parts[slot] = jnp.where(hit, 1.0, 0.0).astype(F32)
    order = sorted(range(10), key=lambda s: BASE[s])
    return jnp.concatenate([parts[s] for s in order], axis=0)


def place_matrix(me, n, so, cl):
    north, south = seam_steps(so, me, n)
    nz, sz = north == 0, south == 0

    def base(zero, slot_a, slot_b):
        return jnp.where(zero, jnp.int32(BASE[slot_a]), jnp.int32(BASE[slot_b]))

    def step(zero, slot_a, slot_b):
        return jnp.where(
            zero, jnp.int32(8 if ROWS[slot_a] == 32 else 4), jnp.int32(8 if ROWS[slot_b] == 32 else 4)
        )

    x = lax.broadcasted_iota(jnp.int32, (16, 256), 0)
    lane = lax.broadcasted_iota(jnp.int32, (16, 256), 1)
    live = [cl[c, me] == 1 for c in range(4)]

    def corner(c, i, j):
        zero, sa, sb = ((nz, 2, 3), (nz, 4, 5), (sz, 6, 7), (sz, 8, 9))[c]
        col = base(zero, sa, sb) + i * step(zero, sa, sb) + j
        return jnp.where(live[c], col, -1)

    blocks = []
    for y in range(14):
        if y < 3:
            left = corner(0, 2 - y, 2 - x)
            mid = base(nz, 3, 4) + (2 - y) * 8 + 10 - x
            right = corner(1, x - 11, 2 - y)
        elif y < 11:
            left = BASE[0] + (2 - x) * 8 + y - 3
            mid = jnp.full_like(x, -1)
            right = BASE[1] + (x - 11) * 8 + 10 - y
        else:
            left = corner(3, 2 - x, y - 11)
            mid = base(sz, 7, 8) + (y - 11) * 8 + x - 3
            right = corner(2, y - 11, x - 11)
        col = jnp.where(x < 3, left, jnp.where(x < 11, mid, jnp.where(x < 14, right, -1)))
        blocks.append(jnp.where(lane == col, 1.0, 0.0).astype(F32))
    blocks.append(jnp.zeros((32, 256), F32))
    return jnp.concatenate(blocks, axis=0)


def whole_wait(ref, sem):
    pltpu.make_async_copy(ref, ref, sem).wait()


def kernel(
    n,
    xin, cot, so_in, sf_in, cf_in, cl_in, dk_in, ng_in, ls_in, win_in, wout_in,
    dx_out, gin_out, gout_out, small_s,
    r1, g2, r2, g3, r3, rz, ag, sm, sr0, s0, sr1, s1, sr2, s2, sr3, s3,
    so, sf, cf, cl, x_s, x0_s, cot_s, s0_m, dk_s, ng_s, ls_s,
    win, wout, pk, s_m, st_m, p_m, pt_m,
    pad, dpad, normed_s, inv_s, mixed_s, before_s, slope_s,
    u_s, h_s, dm_s, db_s, a_s, b_s,
    send_f, recv_f, send_b, recv_b,
    wsem, wsend, pksem, fs_sem, fr_sem, bs_sem, br_sem, psend, precv,
    ms_sem, mr_sem, go_sem, ss_sem, sr_sem, so_sem, in_sem, xr_sem,
):
    seg = lax.axis_index("segment")
    me = lax.axis_index("tile")
    other = 1 - seg

    seams = [
        pltpu.make_async_copy(src, dst, in_sem.at[k])
        for k, (src, dst) in enumerate(((so_in, so), (sf_in, sf), (cf_in, cf), (cl_in, cl)))
    ]
    x_copy = pltpu.make_async_copy(xin.at[seg], x_s, in_sem.at[4])
    small_in = [
        pltpu.make_async_copy(src, dst, in_sem.at[5 + k])
        for k, (src, dst) in enumerate(((dk_in, dk_s), (ng_in, ng_s), (ls_in, ls_s)))
    ]
    for copy in [*seams, x_copy, *small_in]:
        copy.start()

    z = lax.rem(me, NZ)
    y = lax.rem(me // NZ, NY)
    x = me // (NZ * NY)
    at1, at2 = x + seg * (y - x), y + seg * (x - y)
    stride1 = NY * NZ - seg * (NY * NZ - NZ)
    stride2 = NZ + seg * (NY * NZ - NZ)

    def device_of(t):
        row = t // NZ
        hi = row // NY
        lo = row - hi * NY
        lo = lo + lax.rem(hi, 2) * (NY - 1 - 2 * lo)
        return (hi * NY + lo) * NZ + lax.rem(t, NZ)

    odd = lax.rem(x, 2)
    tile = device_of(me)
    mirror = tile

    def peer1(d):
        to = lax.rem(at1 + d, NX)
        return to, me + (to - at1) * stride1

    def peer2(d):
        to = lax.rem(at2 + d, NX)
        return to, me + (to - at2) * stride2

    def peer3(d):
        to = lax.rem(z + d, NZ)
        return to, me + to - z

    barrier = pltpu.get_barrier_semaphore()
    partners = [(seg, peer1(d)[1]) for d in range(1, NX)]
    partners += [(other, peer1(d)[1]) for d in range(1, NX)]
    partners += [(seg, peer2(d)[1]) for d in range(1, NX)]
    partners += [(other, peer2(d)[1]) for d in range(1, NX)]
    partners += [(seg, peer3(d)[1]) for d in range(1, NZ)]
    for off in OFFSETS:
        if abs(off) not in (NZ, 3 * NZ):
            partners.append((seg, lax.rem(tile + off + n, n)))
        partners.append((seg, device_of(lax.rem(tile + off + n, n))))
    partners.append((other, me))
    for partner in partners:
        pl.semaphore_signal(barrier, inc=1, device_id=partner, device_id_type=MESH)

    @pl.when(odd == 1)
    def _():
        pl.semaphore_signal(barrier, inc=1, device_id=(seg, mirror), device_id_type=MESH)

    stays = {off: tile == lax.rem(me - off + n, n) for off in OFFSETS if abs(off) in (NZ, 3 * NZ)}
    signals = len(partners) + odd
    for off, stay in stays.items():
        signals = signals + jnp.where(stay, 0, 1)

        @pl.when(jnp.logical_not(stay))
        def _():
            pl.semaphore_signal(
                barrier, inc=1, device_id=(seg, lax.rem(tile + off + n, n)), device_id_type=MESH
            )

    mine = pl.ds(2 * seg, 2)
    for l in range(2):
        b = 2 * seg + l
        pltpu.make_async_copy(win_in.at[l], win.at[b], wsem.at[0, b]).start()
        pltpu.make_async_copy(wout_in.at[l], wout.at[b], wsem.at[1, b]).start()

    for copy in seams:
        copy.wait()
    s0_m[...] = send_matrix(me, n, so, sf, cf).astype(BF16)
    x_copy.wait()
    send_f[0] = dot(s0_m[...], x_s[...]).astype(BF16)

    for copy in small_in:
        copy.wait()
    taps = dk_s[...].astype(F32)
    for l in range(2):
        b = 2 * seg + l
        pk[b, 0:49, :] = taps[:, l, :]
        pk[b, 49:50, :] = ng_s[l : l + 1, :]
        pk[b, 50:51, :] = ls_s[l : l + 1, :]
        pk[b, 51:64, :] = jnp.zeros((13, C), F32)

    pl.semaphore_wait(barrier, signals)

    first = [device_of(lax.rem(me - off + n, n)) for off in OFFSETS]
    behind = [device_of(lax.rem(tile - off + n, n)) for off in OFFSETS]
    ahead = [device_of(lax.rem(tile + off + n, n)) for off in OFFSETS]

    def exchange(src, dst, ssem, rsem, sign, home):
        for slot in SEND_ORDER:
            off = OFFSETS[slot]
            rows = pl.ds(BASE[slot], ROWS[slot])

            to = ahead[slot] if sign < 0 else behind[slot] if home is tile else first[slot]

            def go():
                pltpu.make_async_remote_copy(
                    src_ref=src.at[rows],
                    dst_ref=dst.at[rows],
                    send_sem=ssem,
                    recv_sem=rsem,
                    device_id=(seg, to),
                    device_id_type=MESH,
                ).start()

            if home is tile or off not in stays:
                go()
            else:
                pl.when(jnp.logical_not(stays[off]))(go)

                @pl.when(stays[off])
                def _():
                    pltpu.make_async_copy(src.at[rows], dst.at[rows], rsem).start()

    def to_partner(src, dst, ssem, rsem):
        return pltpu.make_async_remote_copy(
            src_ref=src, dst_ref=dst, send_sem=ssem, recv_sem=rsem,
            device_id=(other, me), device_id_type=MESH,
        )

    exchange(send_f.at[0], recv_f.at[0], fs_sem.at[0], fr_sem.at[0], 1, me)

    @pl.when(odd == 1)
    def _():
        for k, (src, dst) in enumerate(((xin, x0_s), (cot, cot_s))):
            pltpu.make_async_remote_copy(
                src_ref=src.at[seg], dst_ref=dst, send_sem=xr_sem.at[0, k], recv_sem=xr_sem.at[1, k],
                device_id=(seg, mirror), device_id_type=MESH,
            ).start()

    @pl.when(odd == 0)
    def _():
        for k, (src, dst) in enumerate(((xin, x0_s), (cot, cot_s))):
            pltpu.make_async_copy(src.at[seg], dst, xr_sem.at[1, k]).start()

    pk_copy = to_partner(pk.at[mine], pk.at[mine], pksem.at[0], pksem.at[1])
    pk_copy.start()
    def operands(b, which):
        src, dst = ((u_s, h_s), (dm_s, db_s))[which], (a_s, b_s)[which]
        for kind in range(2):
            at = (x, y)[kind]
            whole = (kind == 0) == (which == 0)
            for d in range(NX):
                to = lax.rem(at + d, NX)
                t = me + (to - at) * (NY * NZ, NZ)[kind]
                part = src[0].at[b] if whole else src[1].at[b, to]
                slot = dst.at[b, 2 * at + seg]

                def go():
                    send(part, slot, psend.at[which, b], precv.at[which, b], (kind, t))

                if d > 0:
                    go()
                else:
                    pl.when(seg != kind)(go)

                    @pl.when(seg == kind)
                    def _():
                        pltpu.make_async_copy(part, slot, precv.at[which, b]).start()

    def send(src, dst, ssem, rsem, device):
        pltpu.make_async_remote_copy(
            src_ref=src, dst_ref=dst, send_sem=ssem, recv_sem=rsem,
            device_id=device, device_id_type=MESH,
        ).start()

    w_copies = []
    for l in range(2):
        b = 2 * seg + l
        w_copies.append(to_partner(win_in.at[l], win.at[b], wsend.at[0, l], wsem.at[0, b]))
        w_copies.append(to_partner(wout_in.at[l], wout.at[b], wsend.at[1, l], wsem.at[1, b]))
    for copy in w_copies:
        copy.start()

    s_f = send_matrix(tile, n, so, sf, cf)
    s_m[...] = s_f.astype(BF16)
    st_m[...] = jnp.transpose(s_f).astype(BF16)
    p_f = place_matrix(tile, n, so, cl)
    p_m[...] = p_f.astype(BF16)
    pt_m[...] = jnp.transpose(p_f).astype(BF16)
    pk_copy.wait()
    whole_wait(x0_s, xr_sem.at[1, 0])
    curb = x0_s[...]

    q1, q2, q3 = 2048 // NX, 2048 // NX // NX, 2048 // NX // NX // NZ
    w1 = 64 // NX

    def main_chain(b):
        l, owner = b % 2, b // 2
        yield
        for which, ref in ((0, a_s), (1, b_s)):
            whole_wait(ref.at[b], precv.at[which, b])
        total = dot(a_s[b].reshape(128 * NX, C), b_s[b].reshape(128 * NX, C), 0, 0)
        for j in range(2):
            g2[b, C * j : C * j + C, :] = total[:, 128 * j : 128 * j + 128].astype(BF16)
        for d in range(1, NX):
            to, t = peer2(d)
            send(g2.at[b, pl.ds(to * q2, q2)], r2.at[b, d - 1], ms_sem.at[1, b], mr_sem.at[1, b], (seg, t))
        yield
        whole_wait(r2.at[b], mr_sem.at[1, b])
        total = g2[b, pl.ds(at2 * q2, q2), :].astype(F32)
        for d in range(NX - 1):
            total = total + r2[b, d].astype(F32)
        g3[b] = total.astype(BF16)
        here2 = pl.ds(at2 * q2, q2)
        if b in SHORT:
            for d in range(1, NZ):
                send(g3.at[b], rz.at[b, d - 1], ms_sem.at[2, b], mr_sem.at[2, b], (seg, peer3(d)[1]))
            yield
            whole_wait(rz.at[b], mr_sem.at[2, b])
            total = g3[b].astype(F32)
            for d in range(NZ - 1):
                total = total + rz[b, d].astype(F32)
            ag[b, here2, :] = total.astype(BF16)
        else:
            for d in range(1, NZ):
                to, t = peer3(d)
                send(g3.at[b, pl.ds(to * q3, q3)], r3.at[b, d - 1], ms_sem.at[2, b], mr_sem.at[2, b], (seg, t))
            yield
            whole_wait(r3.at[b], mr_sem.at[2, b])
            total = g3[b, pl.ds(z * q3, q3), :].astype(F32)
            for d in range(NZ - 1):
                total = total + r3[b, d].astype(F32)
            here = pl.ds(at2 * q2 + z * q3, q3)
            ag[b, here, :] = total.astype(BF16)
            for d in range(1, NZ):
                send(ag.at[b, here], ag.at[b, here], ms_sem.at[3, b], mr_sem.at[3, b], (seg, peer3(d)[1]))
            yield
            whole_wait(ag.at[b, pl.ds(0, (NZ - 1) * q3)], mr_sem.at[3, b])
        for d in range(1, NX):
            send(ag.at[b, here2], ag.at[b, here2], ms_sem.at[4, b], mr_sem.at[4, b], (seg, peer2(d)[1]))
        yield
        whole_wait(ag.at[b, pl.ds(0, (NX - 1) * q2)], mr_sem.at[4, b])
        for kind in range(2):

            @pl.when(seg == kind)
            def _():
                at = pl.multiple_of(at1 * C, 128)
                pairs = []
                for j in range(2):
                    if kind == 0:
                        dst = gin_out.at[l, :, pl.ds(at + 128 * j, 128)]
                    else:
                        dst = gout_out.at[l, pl.ds(at, C), pl.ds(128 * j, 128)]
                    pairs.append((ag.at[b, pl.ds(C * j, C)], dst))
                for d in range(1, NX):
                    for src, dst in pairs:
                        send(src, dst, ms_sem.at[5, b], go_sem.at[l, kind], (owner, peer1(d)[1]))
                for src, dst in pairs:
                    if kind == owner:
                        pltpu.make_async_copy(src, dst, go_sem.at[l, kind]).start()
                    else:
                        send(src, dst, ms_sem.at[6, b], go_sem.at[l, kind], (other, me))

    def small_chain(b):
        l, owner = b % 2, b // 2
        send(sm.at[b, pl.ds(other * 64, 64)], sr0.at[b], ss_sem.at[0, b], sr_sem.at[0, b], (other, me))
        yield
        whole_wait(sr0.at[b], sr_sem.at[0, b])
        s0[b] = sm[b, pl.ds(seg * 64, 64), :] + sr0[b]
        for d in range(1, NX):
            to, t = peer1(d)
            send(s0.at[b, pl.ds(to * w1, w1)], sr1.at[b, d - 1], ss_sem.at[1, b], sr_sem.at[1, b], (seg, t))
        yield
        whole_wait(sr1.at[b], sr_sem.at[1, b])
        s1[b] = s0[b, pl.ds(at1 * w1, w1), :] + jnp.sum(sr1[b], axis=0)
        for d in range(1, NX):
            send(s1.at[b], sr2.at[b, d - 1], ss_sem.at[2, b], sr_sem.at[2, b], (seg, peer2(d)[1]))
        yield
        whole_wait(sr2.at[b], sr_sem.at[2, b])
        s2[b] = s1[b] + jnp.sum(sr2[b], axis=0)
        for d in range(1, NZ):
            send(s2.at[b], sr3.at[b, d - 1], ss_sem.at[3, b], sr_sem.at[3, b], (seg, peer3(d)[1]))
        yield
        whole_wait(sr3.at[b], sr_sem.at[3, b])
        s3[b] = s2[b] + jnp.sum(sr3[b], axis=0)
        out = small_s.at[l, pl.ds(seg * 64 + at1 * w1, w1)]
        for d in range(1, NX):
            send(s3.at[b], out, ss_sem.at[4, b], so_sem.at[l], (owner, peer1(d)[1]))

        @pl.when(seg == owner)
        def _():
            pltpu.make_async_copy(s3.at[b], out, so_sem.at[l]).start()

        @pl.when(seg != owner)
        def _():
            send(s3.at[b], out, ss_sem.at[5, b], so_sem.at[l], (other, me))

    chains = []

    def begin(chain):
        next(chain)
        chains.append(chain)

    def advance(which=None):
        for chain in list(chains if which is None else which):
            if chain in chains and next(chain, True):
                chains.remove(chain)

    def slope_of(b):
        before = before_s[...]
        slope_s[b] = (
            0.5 * (1.0 + lax.erf(before * ROOT_HALF))
            + before * jnp.exp(-0.5 * before * before) * INV_ROOT_TAU
        )

    for b in range(BLOCKS):
        if b > 0:
            send_f[b] = dot(s_m[...], curb).astype(BF16)
            exchange(send_f.at[b], recv_f.at[b], fs_sem.at[b], fr_sem.at[b], 1, tile)
            slope_of(b - 1)
        cur = curb.astype(F32)
        whole_wait(recv_f.at[b], fr_sem.at[b])
        pad[b] = dot(p_m[...], recv_f[b]).reshape(16, 16, C)
        pad[b, 3:11, 3:11, :] = cur.reshape(8, 8, C)
        acc = jnp.zeros((8, 8, C), F32)
        for q in range(7):
            cols = pad[b, 0:14, q : q + 8, :]
            for r in range(7):
                acc = acc + cols[r : r + 8] * pk[b, 7 * r + q : 7 * r + q + 1, :]
        filtered = acc.reshape(64, C)
        centred = filtered - jnp.mean(filtered, axis=-1, keepdims=True)
        inv_std = lax.rsqrt(jnp.mean(centred * centred, axis=-1, keepdims=True) + EPSILON)
        normed = centred * inv_std
        normed_s[b] = normed
        inv_s[b] = jnp.broadcast_to(inv_std, (64, 128))
        unit = (normed * pk[b, 49:50, :]).astype(BF16)
        u_s[b] = unit
        whole_wait(win.at[b], wsem.at[0, b])
        before = dot(unit, win[b])
        before_s[...] = before
        hidden = (0.5 * before * (1.0 + lax.erf(before * ROOT_HALF))).astype(BF16)
        for k in range(NX):
            h_s[b, k] = hidden[:, k * HID // NX : (k + 1) * HID // NX]
        whole_wait(wout.at[b], wsem.at[1, b])
        mixed = dot(hidden, wout[b])
        mixed_s[b] = mixed
        curb = (cur + pk[b, 50:51, :] * mixed).astype(BF16)

        operands(b, 0)

    whole_wait(cot_s, xr_sem.at[1, 1])
    up = cot_s[...].astype(F32)
    slope_of(BLOCKS - 1)
    for b in reversed(range(BLOCKS)):
        dm = (up * pk[b, 50:51, :]).astype(BF16)
        dm_s[b] = dm

        d_hidden = dot(dm, wout[b], 1, 1)
        db = (d_hidden * slope_s[b]).astype(BF16)
        for k in range(NX):
            db_s[b, k] = db[:, k * HID // NX : (k + 1) * HID // NX]
        if b == 0:
            operands(b, 1)
        d_unit = dot(db, win[b], 1, 1)
        normed = normed_s[b]
        inv_std = inv_s[b, :, 0:1]
        dn = d_unit * pk[b, 49:50, :]
        df = inv_std * (
            dn
            - jnp.mean(dn, axis=-1, keepdims=True)
            - normed * jnp.mean(dn * normed, axis=-1, keepdims=True)
        )
        df = df.reshape(8, 8, C)
        older = list(chains)

        def put(row, value):
            sm[b, row : row + 1, :] = value[:, 0:128]
            sm[b, 64 + row : 65 + row, :] = value[:, 128:256]

        def small_grads():
            put(49, jnp.sum(d_unit * normed, axis=0, keepdims=True))
            put(50, jnp.sum(up * mixed_s[b], axis=0, keepdims=True))
            sm[b, 51:64, :] = jnp.zeros((13, 128), F32)
            sm[b, 115:128, :] = jnp.zeros((13, 128), F32)
            for q in range(7):
                cols = pad[b, 0:14, q : q + 8, :]
                for r in range(7):
                    tap = 7 * r + q
                    prod = jnp.sum(df * cols[r : r + 8], axis=0)
                    put(tap, jnp.sum(prod, axis=0, keepdims=True))
            begin(small_chain(b))

        begin(main_chain(b))

        if b == 0:
            small_grads()
        dpad[...] = jnp.zeros((16, 16, C), F32)
        for q in range(7):
            rows = [None] * 14
            for r in range(7):
                term = df * pk[b, 7 * r + q : 7 * r + q + 1, :]
                for i in range(8):
                    part = term[i]
                    rows[r + i] = part if rows[r + i] is None else rows[r + i] + part
            dpad[0:14, q : q + 8, :] += jnp.stack(rows)
        send_b[b] = dot(pt_m[...], dpad[...].reshape(256, C).astype(BF16)).astype(BF16)
        exchange(send_b.at[b], recv_b.at[b], bs_sem.at[b], br_sem.at[b], -1, tile)

        if b > 0:
            operands(b, 1)
        advance(older)
        if b > 0:
            small_grads()
        whole_wait(recv_b.at[b], br_sem.at[b])
        back = dot(st_m[...], recv_b[b])
        up = (up + dpad[3:11, 3:11, :].reshape(64, C) + back).astype(BF16)
        if b == 0:
            x_s[...] = up

            @pl.when(odd == 1)
            def _():
                pltpu.make_async_remote_copy(
                    src_ref=x_s, dst_ref=dx_out, send_sem=xr_sem.at[0, 2], recv_sem=xr_sem.at[1, 2],
                    device_id=(seg, mirror), device_id_type=MESH,
                ).start()

            @pl.when(odd == 0)
            def _():
                pltpu.make_async_copy(x_s, dx_out, xr_sem.at[1, 2]).start()

        up = up.astype(F32)

    while chains:
        advance(chains[::-1])
    for l in range(2):
        whole_wait(small_s.at[l], so_sem.at[l])
        whole_wait(gin_out.at[l], go_sem.at[l, 0])
        whole_wait(gout_out.at[l], go_sem.at[l, 1])
    whole_wait(dx_out, xr_sem.at[1, 2])
    stay = functools.reduce(jnp.logical_or, stays.values())
    kept = 256 - ROWS[OFFSETS.index(next(iter(stays)))]

    @pl.when(stay)
    def _():
        whole_wait(send_f.at[0, pl.ds(0, kept)], fs_sem.at[0])

    @pl.when(jnp.logical_not(stay))
    def _():
        whole_wait(send_f.at[0], fs_sem.at[0])

    @pl.when(odd == 1)
    def _():
        for k in range(3):
            whole_wait(x_s, xr_sem.at[0, k])

    for copy in w_copies:
        copy.wait_send()
    for b in range(BLOCKS):
        if b > 0:
            whole_wait(send_f.at[b], fs_sem.at[b])
        whole_wait(send_b.at[b], bs_sem.at[b])
        for which in range(2):
            whole_wait(a_s.at[b, pl.ds(0, 2 * NX - 1)], psend.at[which, b])
        whole_wait(r2.at[b], ms_sem.at[1, b])
        if b in SHORT:
            whole_wait(rz.at[b], ms_sem.at[2, b])
        else:
            whole_wait(r3.at[b], ms_sem.at[2, b])
            whole_wait(r3.at[b], ms_sem.at[3, b])
        whole_wait(r2.at[b], ms_sem.at[4, b])
        whole_wait(r1.at[b], ms_sem.at[5, b])
        whole_wait(sr0.at[b], ss_sem.at[0, b])
        whole_wait(sr1.at[b], ss_sem.at[1, b])
        whole_wait(sr2.at[b], ss_sem.at[2, b])
        whole_wait(sr3.at[b], ss_sem.at[3, b])
        whole_wait(sr1.at[b], ss_sem.at[4, b])

        @pl.when(seg != b // 2)
        def _():
            whole_wait(ag.at[b], ms_sem.at[6, b])
            whole_wait(s3.at[b], ss_sem.at[5, b])


def finish(
    factor, dx, gin, gout, small, dx_out, gin_out, gout_out, gk_out, gg_out, gs_out,
    in_n, in_w, out_n, out_w, small_n, gk_w, gg_w, gs_w, in_sem, out_sem,
):
    loads, stores, stages = [], [], []
    for src, dst, narrow, wide in ((gin, gin_out, in_n, in_w), (gout, gout_out, out_n, out_w)):
        rows = src.shape[1] // 2
        for l in range(2):
            for h in range(2):
                part = pl.ds(h * rows, rows)
                k = len(loads)
                loads.append(pltpu.make_async_copy(src.at[l, part], narrow.at[l, part], in_sem.at[k]))
                stores.append(pltpu.make_async_copy(wide.at[l, part], dst.at[l, part], out_sem.at[k]))
                stages.append((narrow, wide, l, part))
    first = pltpu.make_async_copy(small, small_n, in_sem.at[8])
    pass_on = pltpu.make_async_copy(dx, dx_out, in_sem.at[9])
    for load in (*loads[:1], first, *loads[1:], pass_on):
        load.start()
    for load, store, (narrow, wide, l, part) in zip(loads, stores, stages):
        load.wait()
        wide[l, part] = narrow[l, part].astype(F32) * factor
        store.start()
    first.wait()
    for l in range(2):
        total = jnp.concatenate([small_n[l, 0:64, :], small_n[l, 64:128, :]], axis=1) * factor
        gk_w[:, l, :] = total[0:49]
        gg_w[l : l + 1, :] = total[49:50]
        gs_w[l : l + 1, :] = total[50:51]
    last = [
        pltpu.make_async_copy(src, dst, out_sem.at[8 + k])
        for k, (src, dst) in enumerate(((gk_w, gk_out), (gg_w, gg_out), (gs_w, gs_out)))
    ]
    for copy in last:
        copy.start()
    for copy in (*stores, *last, pass_on):
        copy.wait()


def local(
    inputs, cotangent, side_owner, side_from, corner_from, corner_live,
    depth_kernel, norm_gain, in_weight, out_weight, layer_scale,
):
    n = lax.axis_size("tile")
    factor = (2 * n * 64) ** (-0.5)
    vmem = pl.BlockSpec(memory_space=pltpu.VMEM)
    hbm = pl.BlockSpec(memory_space=pl.ANY)
    V = pltpu.VMEM
    S = pltpu.SMEM
    shape = jax.ShapeDtypeStruct
    q1, q2, q3 = 2048 // NX, 2048 // NX // NX, 2048 // NX // NX // NZ
    w1 = 64 // NX
    dma = pltpu.SemaphoreType.DMA
    dx, d_in, d_out, small = pl.pallas_call(
        functools.partial(kernel, n),
        out_shape=(
            shape((64, C), BF16), shape((2, C, HID), BF16), shape((2, HID, C), BF16), shape((2, 128, 128), F32),
        ),
        in_specs=[hbm] * 11,
        out_specs=(hbm,) * 4,
        scratch_shapes=[
            V((BLOCKS, NX - 1, q1, 128), BF16), V((BLOCKS, q1, 128), BF16),
            V((BLOCKS, NX - 1, q2, 128), BF16), V((BLOCKS, q2, 128), BF16), V((BLOCKS, NZ - 1, q3, 128), BF16),
            V((BLOCKS, NZ - 1, q2, 128), BF16),
            V((BLOCKS, q1, 128), BF16), V((BLOCKS, 128, 128), F32),
            V((BLOCKS, 64, 128), F32), V((BLOCKS, 64, 128), F32),
            V((BLOCKS, NX - 1, w1, 128), F32), V((BLOCKS, w1, 128), F32),
            V((BLOCKS, NX - 1, w1, 128), F32), V((BLOCKS, w1, 128), F32),
            V((BLOCKS, NZ - 1, w1, 128), F32), V((BLOCKS, w1, 128), F32),
            S((4, n), jnp.int32), S((4, n), jnp.int32), S((4, n), jnp.int32), S((4, n), jnp.int32),
            V((64, C), BF16), V((64, C), BF16), V((64, C), BF16), V((256, 64), BF16),
            V((49, 2, C), BF16), V((2, C), F32), V((2, C), F32),
            V((BLOCKS, C, HID), BF16), V((BLOCKS, HID, C), BF16), V((BLOCKS, SMALL, C), F32),
            V((256, 64), BF16), V((64, 256), BF16), V((256, 256), BF16), V((256, 256), BF16),
            V((BLOCKS, 16, 16, C), F32), V((16, 16, C), F32),
            V((BLOCKS, 64, C), F32), V((BLOCKS, 64, 128), F32), V((BLOCKS, 64, C), F32),
            V((64, HID), F32), V((BLOCKS, 64, HID), F32),
            V((BLOCKS, 64, C), BF16), V((BLOCKS, NX, 64, HID // NX), BF16),
            V((BLOCKS, 64, C), BF16), V((BLOCKS, NX, 64, HID // NX), BF16),
            V((BLOCKS, 2 * NX, 64, C), BF16), V((BLOCKS, 2 * NX, 64, C), BF16),
            V((BLOCKS, 256, C), BF16), V((BLOCKS, 256, C), BF16),
            V((BLOCKS, 256, C), BF16), V((BLOCKS, 256, C), BF16),
            dma((2, BLOCKS)), dma((2, 2)), dma((2,)),
            dma((BLOCKS,)), dma((BLOCKS,)), dma((BLOCKS,)), dma((BLOCKS,)),
            dma((2, BLOCKS)), dma((2, BLOCKS)),
            dma((7, BLOCKS)), dma((5, BLOCKS)), dma((2, 2)), dma((6, BLOCKS)), dma((4, BLOCKS)), dma((2,)),
            dma((8,)), dma((2, 3)),
        ],
        compiler_params=pltpu.CompilerParams(
            collective_id=0, has_side_effects=True, vmem_limit_bytes=VMEM_BYTES
        ),
    )(
        inputs.reshape(2, 64, C), cotangent.reshape(2, 64, C),
        side_owner.T, side_from.T, corner_from.T, corner_live.T,
        depth_kernel.transpose(1, 0, 2), norm_gain, layer_scale, in_weight, out_weight,
    )
    dx, d_in, d_out, d_kernel, d_gain, d_scale = pl.pallas_call(
        functools.partial(finish, factor),
        out_shape=(
            shape((1, 8, 8, C), BF16), shape((2, C, HID), F32), shape((2, HID, C), F32),
            shape((49, 2, C), F32), shape((2, C), F32), shape((2, C), F32),
        ),
        in_specs=[hbm] * 4,
        out_specs=(hbm,) * 6,
        scratch_shapes=[
            V((2, C, HID), BF16), V((2, C, HID), F32), V((2, HID, C), BF16), V((2, HID, C), F32),
            V((2, 128, 128), F32), V((49, 2, C), F32), V((2, C), F32), V((2, C), F32),
            dma((10,)), dma((11,)),
        ],
        compiler_params=pltpu.CompilerParams(vmem_limit_bytes=VMEM_BYTES),
    )(dx.reshape(1, 8, 8, C), d_in, d_out, small)
    return dx, d_kernel.transpose(1, 0, 2), d_gain, d_in, d_out, d_scale


def solution(mesh):
    in_specs = (
        P(None, "tile", None, None), P(None, "tile", None, None),
        P(), P(), P(), P(),
        P("segment", None, None), P("segment", None), P("segment", None, None),
        P("segment", None, None), P("segment", None),
    )
    out_specs = (
        P("segment", "tile", None, None), P("segment", None, None), P("segment", None),
        P("segment", None, None), P("segment", None, None), P("segment", None),
    )
    return jax.shard_map(local, mesh=mesh, in_specs=in_specs, out_specs=out_specs, check_vma=False)
```

```python
import functools

import jax
import jax.numpy as jnp
from jax import lax
from jax.experimental import pallas as pl
from jax.experimental.pallas import tpu as pltpu
from jax.sharding import PartitionSpec as P

GW = 8
BLOCKS = 4
C = 256
HID = 1024
EPSILON = 1e-06
ROOT_HALF = 0.7071067811865476
INV_ROOT_TAU = 0.3989422804014327
MESH = pl.DeviceIdType.MESH
F32 = jnp.float32
BF16 = jnp.bfloat16

OFFSETS = (-1, 1, -GW - 1, -GW, -GW + 1, -GW + 2, GW + 1, GW, GW - 1, GW - 2)
ROWS = (32, 32, 16, 32, 32, 16, 16, 32, 32, 16)
BASE = (0, 32, 192, 64, 96, 208, 224, 128, 160, 240)
SEND_ORDER = (2, 5, 6, 9, 3, 4, 7, 8, 0, 1)
SMALL = 64
NX, NY, NZ = 4, 4, 8
VMEM_BYTES = 60 * 1024 * 1024


def dot(a, b, da=1, db=0):
    return lax.dot_general(a, b, (((da,), (db,)), ((), ())), preferred_element_type=F32)


def pick(code, values):
    out = jnp.int32(values[-1])
    for k in range(len(values) - 2, -1, -1):
        out = jnp.where(code == k, jnp.int32(values[k]), out)
    return out


def seam_steps(so, t, n):
    north = lax.rem(so[0, t] - t + GW + n, n)
    south = lax.rem(t + GW - so[2, t] + n, n)
    return north, south


def wanted_rim(slot, t, so, sf, cf, n):
    north, south = seam_steps(so, t, n)
    if slot == 0:
        return sf[3, t]
    if slot == 1:
        return sf[1, t]
    if slot == 2:
        return cf[0, t]
    if slot == 3:
        return jnp.where(north == 0, sf[0, t], cf[0, t])
    if slot == 4:
        return jnp.where(north == 1, sf[0, t], cf[1, t])
    if slot == 5:
        return cf[1, t]
    if slot == 6:
        return cf[2, t]
    if slot == 7:
        return jnp.where(south == 0, sf[2, t], cf[2, t])
    if slot == 8:
        return jnp.where(south == 1, sf[2, t], cf[3, t])
    return cf[3, t]


def send_matrix(me, n, so, sf, cf):
    parts = [None] * 10
    for slot in range(10):
        rows = ROWS[slot]
        code = wanted_rim(slot, lax.rem(me - OFFSETS[slot] + n, n), so, sf, cf, n)
        a = pick(code, (0, 7, 63, 56))
        b = pick(code, (8, -1, -8, 1))
        d = pick(code, (1, 8, -1, -8))
        row = lax.broadcasted_iota(jnp.int32, (rows, 64), 0)
        pixel = lax.broadcasted_iota(jnp.int32, (rows, 64), 1)
        if rows == 32:
            i, j = row >> 3, row & 7
            valid = row < 24
        else:
            i, j = row >> 2, row & 3
            valid = (row < 12) & (j < 3)
        hit = (pixel == a + b * i + d * j) & valid
        parts[slot] = jnp.where(hit, 1.0, 0.0).astype(F32)
    order = sorted(range(10), key=lambda s: BASE[s])
    return jnp.concatenate([parts[s] for s in order], axis=0)


def place_matrix(me, n, so, cl):
    north, south = seam_steps(so, me, n)
    nz, sz = north == 0, south == 0

    def base(zero, slot_a, slot_b):
        return jnp.where(zero, jnp.int32(BASE[slot_a]), jnp.int32(BASE[slot_b]))

    def step(zero, slot_a, slot_b):
        return jnp.where(
            zero, jnp.int32(8 if ROWS[slot_a] == 32 else 4), jnp.int32(8 if ROWS[slot_b] == 32 else 4)
        )

    x = lax.broadcasted_iota(jnp.int32, (16, 256), 0)
    lane = lax.broadcasted_iota(jnp.int32, (16, 256), 1)
    live = [cl[c, me] == 1 for c in range(4)]

    def corner(c, i, j):
        zero, sa, sb = ((nz, 2, 3), (nz, 4, 5), (sz, 6, 7), (sz, 8, 9))[c]
        col = base(zero, sa, sb) + i * step(zero, sa, sb) + j
        return jnp.where(live[c], col, -1)

    blocks = []
    for y in range(14):
        if y < 3:
            left = corner(0, 2 - y, 2 - x)
            mid = base(nz, 3, 4) + (2 - y) * 8 + 10 - x
            right = corner(1, x - 11, 2 - y)
        elif y < 11:
            left = BASE[0] + (2 - x) * 8 + y - 3
            mid = jnp.full_like(x, -1)
            right = BASE[1] + (x - 11) * 8 + 10 - y
        else:
            left = corner(3, 2 - x, y - 11)
            mid = base(sz, 7, 8) + (y - 11) * 8 + x - 3
            right = corner(2, y - 11, x - 11)
        col = jnp.where(x < 3, left, jnp.where(x < 11, mid, jnp.where(x < 14, right, -1)))
        blocks.append(jnp.where(lane == col, 1.0, 0.0).astype(F32))
    blocks.append(jnp.zeros((32, 256), F32))
    return jnp.concatenate(blocks, axis=0)


def whole_wait(ref, sem):
    pltpu.make_async_copy(ref, ref, sem).wait()


def kernel(
    n,
    xin, cot, so_in, sf_in, cf_in, cl_in, dk_in, ng_in, ls_in, win_in, wout_in,
    dx_out, gin_out, gout_out, small_s,
    r1, g2, r2, g3, r3, ag, sm, sr0, s0, sr1, s1, sr2, s2, sr3, s3,
    so, sf, cf, cl, x_s, x0_s, cot_s, s0_m, dk_s, ng_s, ls_s,
    win, wout, win_t, wout_t, pk, s_m, st_m, p_m, pt_m,
    pad, dpad, normed_s, inv_s, mixed_s, before_s, slope_s,
    u_s, h_s, dm_s, db_s, a_s, b_s,
    send_f, recv_f, send_b, recv_b,
    wsem, wsend, pksem, fs_sem, fr_sem, bs_sem, br_sem, psend, precv,
    ms_sem, mr_sem, go_sem, ss_sem, sr_sem, so_sem, in_sem, xr_sem,
):
    seg = lax.axis_index("segment")
    me = lax.axis_index("tile")
    other = 1 - seg

    seams = [
        pltpu.make_async_copy(src, dst, in_sem.at[k])
        for k, (src, dst) in enumerate(((so_in, so), (sf_in, sf), (cf_in, cf), (cl_in, cl)))
    ]
    x_copy = pltpu.make_async_copy(xin.at[seg], x_s, in_sem.at[4])
    small_in = [
        pltpu.make_async_copy(src, dst, in_sem.at[5 + k])
        for k, (src, dst) in enumerate(((dk_in, dk_s), (ng_in, ng_s), (ls_in, ls_s)))
    ]
    for copy in [*seams, x_copy, *small_in]:
        copy.start()

    z = lax.rem(me, NZ)
    y = lax.rem(me // NZ, NY)
    x = me // (NZ * NY)
    at1, at2 = x + seg * (y - x), y + seg * (x - y)
    stride1 = NY * NZ - seg * (NY * NZ - NZ)
    stride2 = NZ + seg * (NY * NZ - NZ)

    def device_of(t):
        row = t // NZ
        hi = row // NY
        lo = row - hi * NY
        lo = lo + lax.rem(hi, 2) * (NY - 1 - 2 * lo)
        return (hi * NY + lo) * NZ + lax.rem(t, NZ)

    odd = lax.rem(x, 2)
    tile = device_of(me)
    mirror = tile

    def peer1(d):
        to = lax.rem(at1 + d, NX)
        return to, me + (to - at1) * stride1

    def peer2(d):
        to = lax.rem(at2 + d, NX)
        return to, me + (to - at2) * stride2

    def peer3(d):
        to = lax.rem(z + d, NZ)
        return to, me + to - z

    barrier = pltpu.get_barrier_semaphore()
    partners = [(seg, peer1(d)[1]) for d in range(1, NX)]
    partners += [(other, peer1(d)[1]) for d in range(1, NX)]
    partners += [(seg, peer2(d)[1]) for d in range(1, NX)]
    partners += [(other, peer2(d)[1]) for d in range(1, NX)]
    partners += [(seg, peer3(d)[1]) for d in range(1, NZ)]
    for off in OFFSETS:
        if abs(off) not in (NZ, 3 * NZ):
            partners.append((seg, lax.rem(tile + off + n, n)))
        partners.append((seg, device_of(lax.rem(tile + off + n, n))))
    partners.append((other, me))
    for partner in partners:
        pl.semaphore_signal(barrier, inc=1, device_id=partner, device_id_type=MESH)

    @pl.when(odd == 1)
    def _():
        pl.semaphore_signal(barrier, inc=1, device_id=(seg, mirror), device_id_type=MESH)

    stays = {off: tile == lax.rem(me - off + n, n) for off in OFFSETS if abs(off) in (NZ, 3 * NZ)}
    signals = len(partners) + odd
    for off, stay in stays.items():
        signals = signals + jnp.where(stay, 0, 1)

        @pl.when(jnp.logical_not(stay))
        def _():
            pl.semaphore_signal(
                barrier, inc=1, device_id=(seg, lax.rem(tile + off + n, n)), device_id_type=MESH
            )

    mine = pl.ds(2 * seg, 2)
    for l in range(2):
        b = 2 * seg + l
        pltpu.make_async_copy(win_in.at[l], win.at[b], wsem.at[0, b]).start()
        pltpu.make_async_copy(wout_in.at[l], wout.at[b], wsem.at[1, b]).start()

    for copy in seams:
        copy.wait()
    s0_m[...] = send_matrix(me, n, so, sf, cf).astype(BF16)
    x_copy.wait()
    send_f[0] = dot(s0_m[...], x_s[...]).astype(BF16)

    for copy in small_in:
        copy.wait()
    taps = dk_s[...].astype(F32)
    for l in range(2):
        b = 2 * seg + l
        pk[b, 0:49, :] = taps[:, l, :]
        pk[b, 49:50, :] = ng_s[l : l + 1, :]
        pk[b, 50:51, :] = ls_s[l : l + 1, :]
        pk[b, 51:64, :] = jnp.zeros((13, C), F32)

    pl.semaphore_wait(barrier, signals)

    first = [device_of(lax.rem(me - off + n, n)) for off in OFFSETS]
    behind = [device_of(lax.rem(tile - off + n, n)) for off in OFFSETS]
    ahead = [device_of(lax.rem(tile + off + n, n)) for off in OFFSETS]

    def exchange(src, dst, ssem, rsem, sign, home):
        for slot in SEND_ORDER:
            off = OFFSETS[slot]
            rows = pl.ds(BASE[slot], ROWS[slot])

            to = ahead[slot] if sign < 0 else behind[slot] if home is tile else first[slot]

            def go():
                pltpu.make_async_remote_copy(
                    src_ref=src.at[rows],
                    dst_ref=dst.at[rows],
                    send_sem=ssem,
                    recv_sem=rsem,
                    device_id=(seg, to),
                    device_id_type=MESH,
                ).start()

            if home is tile or off not in stays:
                go()
            else:
                pl.when(jnp.logical_not(stays[off]))(go)

                @pl.when(stays[off])
                def _():
                    pltpu.make_async_copy(src.at[rows], dst.at[rows], rsem).start()

    def to_partner(src, dst, ssem, rsem):
        return pltpu.make_async_remote_copy(
            src_ref=src, dst_ref=dst, send_sem=ssem, recv_sem=rsem,
            device_id=(other, me), device_id_type=MESH,
        )

    exchange(send_f.at[0], recv_f.at[0], fs_sem.at[0], fr_sem.at[0], 1, me)

    @pl.when(odd == 1)
    def _():
        for k, (src, dst) in enumerate(((xin, x0_s), (cot, cot_s))):
            pltpu.make_async_remote_copy(
                src_ref=src.at[seg], dst_ref=dst, send_sem=xr_sem.at[0, k], recv_sem=xr_sem.at[1, k],
                device_id=(seg, mirror), device_id_type=MESH,
            ).start()

    @pl.when(odd == 0)
    def _():
        for k, (src, dst) in enumerate(((xin, x0_s), (cot, cot_s))):
            pltpu.make_async_copy(src.at[seg], dst, xr_sem.at[1, k]).start()

    pk_copy = to_partner(pk.at[mine], pk.at[mine], pksem.at[0], pksem.at[1])
    pk_copy.start()
    def operands(b, which):
        src, dst = ((u_s, h_s), (dm_s, db_s))[which], (a_s, b_s)[which]
        for kind in range(2):
            at = (x, y)[kind]
            whole = (kind == 0) == (which == 0)
            for d in range(NX):
                to = lax.rem(at + d, NX)
                t = me + (to - at) * (NY * NZ, NZ)[kind]
                part = src[0].at[b] if whole else src[1].at[b, to]
                slot = dst.at[b, 2 * at + seg]

                def go():
                    send(part, slot, psend.at[which, b], precv.at[which, b], (kind, t))

                if d > 0:
                    go()
                else:
                    pl.when(seg != kind)(go)

                    @pl.when(seg == kind)
                    def _():
                        pltpu.make_async_copy(part, slot, precv.at[which, b]).start()

    def send(src, dst, ssem, rsem, device):
        pltpu.make_async_remote_copy(
            src_ref=src, dst_ref=dst, send_sem=ssem, recv_sem=rsem,
            device_id=device, device_id_type=MESH,
        ).start()

    w_copies = []
    for l in range(2):
        b = 2 * seg + l
        w_copies.append(to_partner(win_in.at[l], win.at[b], wsend.at[0, l], wsem.at[0, b]))
        w_copies.append(to_partner(wout_in.at[l], wout.at[b], wsend.at[1, l], wsem.at[1, b]))
    for copy in w_copies:
        copy.start()

    s_f = send_matrix(tile, n, so, sf, cf)
    s_m[...] = s_f.astype(BF16)
    st_m[...] = jnp.transpose(s_f).astype(BF16)
    p_f = place_matrix(tile, n, so, cl)
    p_m[...] = p_f.astype(BF16)
    pt_m[...] = jnp.transpose(p_f).astype(BF16)
    pk_copy.wait()
    whole_wait(x0_s, xr_sem.at[1, 0])
    curb = x0_s[...]

    q1, q2, q3 = 2048 // NX, 2048 // NX // NX, 2048 // NX // NX // NZ
    w1 = 64 // NX

    def main_chain(b):
        l, owner = b % 2, b // 2
        yield
        for which, ref in ((0, a_s), (1, b_s)):
            whole_wait(ref.at[b], precv.at[which, b])
        total = dot(a_s[b].reshape(128 * NX, C), b_s[b].reshape(128 * NX, C), 0, 0)
        for j in range(2):
            g2[b, C * j : C * j + C, :] = total[:, 128 * j : 128 * j + 128].astype(BF16)
        for d in range(1, NX):
            to, t = peer2(d)
            send(g2.at[b, pl.ds(to * q2, q2)], r2.at[b, d - 1], ms_sem.at[1, b], mr_sem.at[1, b], (seg, t))
        yield
        whole_wait(r2.at[b], mr_sem.at[1, b])
        total = g2[b, pl.ds(at2 * q2, q2), :].astype(F32)
        for d in range(NX - 1):
            total = total + r2[b, d].astype(F32)
        g3[b] = total.astype(BF16)
        here2 = pl.ds(at2 * q2, q2)
        for d in range(1, NZ):
            to, t = peer3(d)
            send(g3.at[b, pl.ds(to * q3, q3)], r3.at[b, d - 1], ms_sem.at[2, b], mr_sem.at[2, b], (seg, t))
        yield
        whole_wait(r3.at[b], mr_sem.at[2, b])
        total = g3[b, pl.ds(z * q3, q3), :].astype(F32)
        for d in range(NZ - 1):
            total = total + r3[b, d].astype(F32)
        here = pl.ds(at2 * q2 + z * q3, q3)
        ag[b, here, :] = total.astype(BF16)
        for d in range(1, NZ):
            send(ag.at[b, here], ag.at[b, here], ms_sem.at[3, b], mr_sem.at[3, b], (seg, peer3(d)[1]))
        yield
        whole_wait(ag.at[b, pl.ds(0, (NZ - 1) * q3)], mr_sem.at[3, b])
        for d in range(1, NX):
            send(ag.at[b, here2], ag.at[b, here2], ms_sem.at[4, b], mr_sem.at[4, b], (seg, peer2(d)[1]))
        yield
        whole_wait(ag.at[b, pl.ds(0, (NX - 1) * q2)], mr_sem.at[4, b])
        for kind in range(2):

            @pl.when(seg == kind)
            def _():
                at = pl.multiple_of(at1 * C, 128)
                pairs = []
                for j in range(2):
                    if kind == 0:
                        dst = gin_out.at[l, :, pl.ds(at + 128 * j, 128)]
                    else:
                        dst = gout_out.at[l, pl.ds(at, C), pl.ds(128 * j, 128)]
                    pairs.append((ag.at[b, pl.ds(C * j, C)], dst))
                for d in range(1, NX):
                    for src, dst in pairs:
                        send(src, dst, ms_sem.at[5, b], go_sem.at[l, kind], (owner, peer1(d)[1]))
                for src, dst in pairs:
                    if kind == owner:
                        pltpu.make_async_copy(src, dst, go_sem.at[l, kind]).start()
                    else:
                        send(src, dst, ms_sem.at[6, b], go_sem.at[l, kind], (other, me))

    def small_chain(b):
        l, owner = b % 2, b // 2
        send(sm.at[b, pl.ds(other * 64, 64)], sr0.at[b], ss_sem.at[0, b], sr_sem.at[0, b], (other, me))
        yield
        whole_wait(sr0.at[b], sr_sem.at[0, b])
        s0[b] = sm[b, pl.ds(seg * 64, 64), :] + sr0[b]
        for d in range(1, NX):
            to, t = peer1(d)
            send(s0.at[b, pl.ds(to * w1, w1)], sr1.at[b, d - 1], ss_sem.at[1, b], sr_sem.at[1, b], (seg, t))
        yield
        whole_wait(sr1.at[b], sr_sem.at[1, b])
        s1[b] = s0[b, pl.ds(at1 * w1, w1), :] + jnp.sum(sr1[b], axis=0)
        for d in range(1, NX):
            send(s1.at[b], sr2.at[b, d - 1], ss_sem.at[2, b], sr_sem.at[2, b], (seg, peer2(d)[1]))
        yield
        whole_wait(sr2.at[b], sr_sem.at[2, b])
        s2[b] = s1[b] + jnp.sum(sr2[b], axis=0)
        for d in range(1, NZ):
            send(s2.at[b], sr3.at[b, d - 1], ss_sem.at[3, b], sr_sem.at[3, b], (seg, peer3(d)[1]))
        yield
        whole_wait(sr3.at[b], sr_sem.at[3, b])
        s3[b] = s2[b] + jnp.sum(sr3[b], axis=0)
        out = small_s.at[l, pl.ds(seg * 64 + at1 * w1, w1)]
        for d in range(1, NX):
            send(s3.at[b], out, ss_sem.at[4, b], so_sem.at[l], (owner, peer1(d)[1]))

        @pl.when(seg == owner)
        def _():
            pltpu.make_async_copy(s3.at[b], out, so_sem.at[l]).start()

        @pl.when(seg != owner)
        def _():
            send(s3.at[b], out, ss_sem.at[5, b], so_sem.at[l], (other, me))

    chains = []

    def begin(chain):
        next(chain)
        chains.append(chain)

    def advance(which=None):
        for chain in list(chains if which is None else which):
            if chain in chains and next(chain, True):
                chains.remove(chain)

    def slope_of(b):
        before = before_s[...]
        slope_s[b] = (
            0.5 * (1.0 + lax.erf(before * ROOT_HALF))
            + before * jnp.exp(-0.5 * before * before) * INV_ROOT_TAU
        )

    def turn(b):
        win_t[b] = jnp.transpose(win[b])
        wout_t[b] = jnp.transpose(wout[b])

    for b in range(BLOCKS):
        if b > 0:
            send_f[b] = dot(s_m[...], curb).astype(BF16)
            exchange(send_f.at[b], recv_f.at[b], fs_sem.at[b], fr_sem.at[b], 1, tile)
            slope_of(b - 1)
            turn(b - 1)
        cur = curb.astype(F32)
        whole_wait(recv_f.at[b], fr_sem.at[b])
        pad[b] = dot(p_m[...], recv_f[b]).reshape(16, 16, C)
        pad[b, 3:11, 3:11, :] = cur.reshape(8, 8, C)
        acc = jnp.zeros((8, 8, C), F32)
        for q in range(7):
            cols = pad[b, 0:14, q : q + 8, :]
            for r in range(7):
                acc = acc + cols[r : r + 8] * pk[b, 7 * r + q : 7 * r + q + 1, :]
        filtered = acc.reshape(64, C)
        centred = filtered - jnp.mean(filtered, axis=-1, keepdims=True)
        inv_std = lax.rsqrt(jnp.mean(centred * centred, axis=-1, keepdims=True) + EPSILON)
        normed = centred * inv_std
        normed_s[b] = normed
        inv_s[b] = jnp.broadcast_to(inv_std, (64, 128))
        unit = (normed * pk[b, 49:50, :]).astype(BF16)
        u_s[b] = unit
        whole_wait(win.at[b], wsem.at[0, b])
        before = dot(unit, win[b])
        before_s[...] = before
        hidden = (0.5 * before * (1.0 + lax.erf(before * ROOT_HALF))).astype(BF16)
        for k in range(NX):
            h_s[b, k] = hidden[:, k * HID // NX : (k + 1) * HID // NX]
        whole_wait(wout.at[b], wsem.at[1, b])
        mixed = dot(hidden, wout[b])
        mixed_s[b] = mixed
        curb = (cur + pk[b, 50:51, :] * mixed).astype(BF16)

        operands(b, 0)

    whole_wait(cot_s, xr_sem.at[1, 1])
    up = cot_s[...].astype(F32)
    slope_of(BLOCKS - 1)
    for b in reversed(range(BLOCKS)):
        dm = (up * pk[b, 50:51, :]).astype(BF16)
        dm_s[b] = dm

        d_hidden = dot(dm, wout_t[b]) if b < BLOCKS - 1 else dot(dm, wout[b], 1, 1)
        db = (d_hidden * slope_s[b]).astype(BF16)
        for k in range(NX):
            db_s[b, k] = db[:, k * HID // NX : (k + 1) * HID // NX]
        if b == 0:
            operands(b, 1)
        d_unit = dot(db, win_t[b]) if b < BLOCKS - 1 else dot(db, win[b], 1, 1)
        normed = normed_s[b]
        inv_std = inv_s[b, :, 0:1]
        dn = d_unit * pk[b, 49:50, :]
        df = inv_std * (
            dn
            - jnp.mean(dn, axis=-1, keepdims=True)
            - normed * jnp.mean(dn * normed, axis=-1, keepdims=True)
        )
        df = df.reshape(8, 8, C)
        older = list(chains)

        def put(row, value):
            sm[b, row : row + 1, :] = value[:, 0:128]
            sm[b, 64 + row : 65 + row, :] = value[:, 128:256]

        def small_grads():
            put(49, jnp.sum(d_unit * normed, axis=0, keepdims=True))
            put(50, jnp.sum(up * mixed_s[b], axis=0, keepdims=True))
            sm[b, 51:64, :] = jnp.zeros((13, 128), F32)
            sm[b, 115:128, :] = jnp.zeros((13, 128), F32)
            for q in range(7):
                cols = pad[b, 0:14, q : q + 8, :]
                for r in range(7):
                    tap = 7 * r + q
                    prod = jnp.sum(df * cols[r : r + 8], axis=0)
                    put(tap, jnp.sum(prod, axis=0, keepdims=True))
            begin(small_chain(b))

        begin(main_chain(b))

        if b == 0:
            small_grads()
        dpad[...] = jnp.zeros((16, 16, C), F32)
        for q in range(7):
            rows = [None] * 14
            for r in range(7):
                term = df * pk[b, 7 * r + q : 7 * r + q + 1, :]
                for i in range(8):
                    part = term[i]
                    rows[r + i] = part if rows[r + i] is None else rows[r + i] + part
            dpad[0:14, q : q + 8, :] += jnp.stack(rows)
        send_b[b] = dot(pt_m[...], dpad[...].reshape(256, C).astype(BF16)).astype(BF16)
        exchange(send_b.at[b], recv_b.at[b], bs_sem.at[b], br_sem.at[b], -1, tile)

        if b > 0:
            operands(b, 1)
        advance(older)
        if b > 0:
            small_grads()
        whole_wait(recv_b.at[b], br_sem.at[b])
        back = dot(st_m[...], recv_b[b])
        up = (up + dpad[3:11, 3:11, :].reshape(64, C) + back).astype(BF16)
        if b == 0:
            x_s[...] = up

            @pl.when(odd == 1)
            def _():
                pltpu.make_async_remote_copy(
                    src_ref=x_s, dst_ref=dx_out, send_sem=xr_sem.at[0, 2], recv_sem=xr_sem.at[1, 2],
                    device_id=(seg, mirror), device_id_type=MESH,
                ).start()

            @pl.when(odd == 0)
            def _():
                pltpu.make_async_copy(x_s, dx_out, xr_sem.at[1, 2]).start()

        up = up.astype(F32)

    while chains:
        advance(chains[::-1])
    for l in range(2):
        whole_wait(small_s.at[l], so_sem.at[l])
        whole_wait(gin_out.at[l], go_sem.at[l, 0])
        whole_wait(gout_out.at[l], go_sem.at[l, 1])
    whole_wait(dx_out, xr_sem.at[1, 2])
    stay = functools.reduce(jnp.logical_or, stays.values())
    kept = 256 - ROWS[OFFSETS.index(next(iter(stays)))]

    @pl.when(stay)
    def _():
        whole_wait(send_f.at[0, pl.ds(0, kept)], fs_sem.at[0])

    @pl.when(jnp.logical_not(stay))
    def _():
        whole_wait(send_f.at[0], fs_sem.at[0])

    @pl.when(odd == 1)
    def _():
        for k in range(3):
            whole_wait(x_s, xr_sem.at[0, k])

    for copy in w_copies:
        copy.wait_send()
    for b in range(BLOCKS):
        if b > 0:
            whole_wait(send_f.at[b], fs_sem.at[b])
        whole_wait(send_b.at[b], bs_sem.at[b])
        for which in range(2):
            whole_wait(a_s.at[b, pl.ds(0, 2 * NX - 1)], psend.at[which, b])
        whole_wait(r2.at[b], ms_sem.at[1, b])
        whole_wait(r3.at[b], ms_sem.at[2, b])
        whole_wait(r3.at[b], ms_sem.at[3, b])
        whole_wait(r2.at[b], ms_sem.at[4, b])
        whole_wait(r1.at[b], ms_sem.at[5, b])
        whole_wait(sr0.at[b], ss_sem.at[0, b])
        whole_wait(sr1.at[b], ss_sem.at[1, b])
        whole_wait(sr2.at[b], ss_sem.at[2, b])
        whole_wait(sr3.at[b], ss_sem.at[3, b])
        whole_wait(sr1.at[b], ss_sem.at[4, b])

        @pl.when(seg != b // 2)
        def _():
            whole_wait(ag.at[b], ms_sem.at[6, b])
            whole_wait(s3.at[b], ss_sem.at[5, b])


def finish(
    factor, dx, gin, gout, small, dx_out, gin_out, gout_out, gk_out, gg_out, gs_out,
    in_n, in_w, out_n, out_w, small_n, gk_w, gg_w, gs_w, in_sem, out_sem,
):
    loads, stores, stages = [], [], []
    for src, dst, narrow, wide in ((gin, gin_out, in_n, in_w), (gout, gout_out, out_n, out_w)):
        rows = src.shape[1] // 2
        for l in range(2):
            for h in range(2):
                part = pl.ds(h * rows, rows)
                k = len(loads)
                loads.append(pltpu.make_async_copy(src.at[l, part], narrow.at[l, part], in_sem.at[k]))
                stores.append(pltpu.make_async_copy(wide.at[l, part], dst.at[l, part], out_sem.at[k]))
                stages.append((narrow, wide, l, part))
    first = pltpu.make_async_copy(small, small_n, in_sem.at[8])
    pass_on = pltpu.make_async_copy(dx, dx_out, in_sem.at[9])
    for load in (*loads[:1], first, *loads[1:], pass_on):
        load.start()
    for load, store, (narrow, wide, l, part) in zip(loads, stores, stages):
        load.wait()
        wide[l, part] = narrow[l, part].astype(F32) * factor
        store.start()
    first.wait()
    for l in range(2):
        total = jnp.concatenate([small_n[l, 0:64, :], small_n[l, 64:128, :]], axis=1) * factor
        gk_w[:, l, :] = total[0:49]
        gg_w[l : l + 1, :] = total[49:50]
        gs_w[l : l + 1, :] = total[50:51]
    last = [
        pltpu.make_async_copy(src, dst, out_sem.at[8 + k])
        for k, (src, dst) in enumerate(((gk_w, gk_out), (gg_w, gg_out), (gs_w, gs_out)))
    ]
    for copy in last:
        copy.start()
    for copy in (*stores, *last, pass_on):
        copy.wait()


def local(
    inputs, cotangent, side_owner, side_from, corner_from, corner_live,
    depth_kernel, norm_gain, in_weight, out_weight, layer_scale,
):
    n = lax.axis_size("tile")
    factor = (2 * n * 64) ** (-0.5)
    vmem = pl.BlockSpec(memory_space=pltpu.VMEM)
    hbm = pl.BlockSpec(memory_space=pl.ANY)
    V = pltpu.VMEM
    S = pltpu.SMEM
    shape = jax.ShapeDtypeStruct
    q1, q2, q3 = 2048 // NX, 2048 // NX // NX, 2048 // NX // NX // NZ
    w1 = 64 // NX
    dma = pltpu.SemaphoreType.DMA
    dx, d_in, d_out, small = pl.pallas_call(
        functools.partial(kernel, n),
        out_shape=(
            shape((64, C), BF16), shape((2, C, HID), BF16), shape((2, HID, C), BF16), shape((2, 128, 128), F32),
        ),
        in_specs=[hbm] * 11,
        out_specs=(hbm,) * 4,
        scratch_shapes=[
            V((BLOCKS, NX - 1, q1, 128), BF16), V((BLOCKS, q1, 128), BF16),
            V((BLOCKS, NX - 1, q2, 128), BF16), V((BLOCKS, q2, 128), BF16), V((BLOCKS, NZ - 1, q3, 128), BF16),
            V((BLOCKS, q1, 128), BF16), V((BLOCKS, 128, 128), F32),
            V((BLOCKS, 64, 128), F32), V((BLOCKS, 64, 128), F32),
            V((BLOCKS, NX - 1, w1, 128), F32), V((BLOCKS, w1, 128), F32),
            V((BLOCKS, NX - 1, w1, 128), F32), V((BLOCKS, w1, 128), F32),
            V((BLOCKS, NZ - 1, w1, 128), F32), V((BLOCKS, w1, 128), F32),
            S((4, n), jnp.int32), S((4, n), jnp.int32), S((4, n), jnp.int32), S((4, n), jnp.int32),
            V((64, C), BF16), V((64, C), BF16), V((64, C), BF16), V((256, 64), BF16),
            V((49, 2, C), BF16), V((2, C), F32), V((2, C), F32),
            V((BLOCKS, C, HID), BF16), V((BLOCKS, HID, C), BF16),
            V((BLOCKS - 1, HID, C), BF16), V((BLOCKS - 1, C, HID), BF16), V((BLOCKS, SMALL, C), F32),
            V((256, 64), BF16), V((64, 256), BF16), V((256, 256), BF16), V((256, 256), BF16),
            V((BLOCKS, 16, 16, C), F32), V((16, 16, C), F32),
            V((BLOCKS, 64, C), F32), V((BLOCKS, 64, 128), F32), V((BLOCKS, 64, C), F32),
            V((64, HID), F32), V((BLOCKS, 64, HID), F32),
            V((BLOCKS, 64, C), BF16), V((BLOCKS, NX, 64, HID // NX), BF16),
            V((BLOCKS, 64, C), BF16), V((BLOCKS, NX, 64, HID // NX), BF16),
            V((BLOCKS, 2 * NX, 64, C), BF16), V((BLOCKS, 2 * NX, 64, C), BF16),
            V((BLOCKS, 256, C), BF16), V((BLOCKS, 256, C), BF16),
            V((BLOCKS, 256, C), BF16), V((BLOCKS, 256, C), BF16),
            dma((2, BLOCKS)), dma((2, 2)), dma((2,)),
            dma((BLOCKS,)), dma((BLOCKS,)), dma((BLOCKS,)), dma((BLOCKS,)),
            dma((2, BLOCKS)), dma((2, BLOCKS)),
            dma((7, BLOCKS)), dma((5, BLOCKS)), dma((2, 2)), dma((6, BLOCKS)), dma((4, BLOCKS)), dma((2,)),
            dma((8,)), dma((2, 3)),
        ],
        compiler_params=pltpu.CompilerParams(
            collective_id=0, has_side_effects=True, vmem_limit_bytes=VMEM_BYTES
        ),
    )(
        inputs.reshape(2, 64, C), cotangent.reshape(2, 64, C),
        side_owner.T, side_from.T, corner_from.T, corner_live.T,
        depth_kernel.transpose(1, 0, 2), norm_gain, layer_scale, in_weight, out_weight,
    )
    dx, d_in, d_out, d_kernel, d_gain, d_scale = pl.pallas_call(
        functools.partial(finish, factor),
        out_shape=(
            shape((1, 8, 8, C), BF16), shape((2, C, HID), F32), shape((2, HID, C), F32),
            shape((49, 2, C), F32), shape((2, C), F32), shape((2, C), F32),
        ),
        in_specs=[hbm] * 4,
        out_specs=(hbm,) * 6,
        scratch_shapes=[
            V((2, C, HID), BF16), V((2, C, HID), F32), V((2, HID, C), BF16), V((2, HID, C), F32),
            V((2, 128, 128), F32), V((49, 2, C), F32), V((2, C), F32), V((2, C), F32),
            dma((10,)), dma((11,)),
        ],
        compiler_params=pltpu.CompilerParams(vmem_limit_bytes=VMEM_BYTES),
    )(dx.reshape(1, 8, 8, C), d_in, d_out, small)
    return dx, d_kernel.transpose(1, 0, 2), d_gain, d_in, d_out, d_scale


def solution(mesh):
    in_specs = (
        P(None, "tile", None, None), P(None, "tile", None, None),
        P(), P(), P(), P(),
        P("segment", None, None), P("segment", None), P("segment", None, None),
        P("segment", None, None), P("segment", None),
    )
    out_specs = (
        P("segment", "tile", None, None), P("segment", None, None), P("segment", None),
        P("segment", None, None), P("segment", None, None), P("segment", None),
    )
    return jax.shard_map(local, mesh=mesh, in_specs=in_specs, out_specs=out_specs, check_vma=False)
```

```python
import functools

import jax
import jax.numpy as jnp
from jax import lax
from jax.experimental import pallas as pl
from jax.experimental.pallas import tpu as pltpu
from jax.sharding import PartitionSpec as P

GW = 8
BLOCKS = 4
C = 256
HID = 1024
EPSILON = 1e-06
ROOT_HALF = 0.7071067811865476
INV_ROOT_TAU = 0.3989422804014327
MESH = pl.DeviceIdType.MESH
F32 = jnp.float32
BF16 = jnp.bfloat16

OFFSETS = (-1, 1, -GW - 1, -GW, -GW + 1, -GW + 2, GW + 1, GW, GW - 1, GW - 2)
ROWS = (32, 32, 16, 32, 32, 16, 16, 32, 32, 16)
BASE = (0, 32, 192, 64, 96, 208, 224, 128, 160, 240)
SEND_ORDER = (2, 5, 6, 9, 3, 4, 7, 8, 0, 1)
SMALL = 64
NX, NY, NZ = 4, 4, 8
VMEM_BYTES = 60 * 1024 * 1024


def dot(a, b, da=1, db=0):
    return lax.dot_general(a, b, (((da,), (db,)), ((), ())), preferred_element_type=F32)


def pick(code, values):
    out = jnp.int32(values[-1])
    for k in range(len(values) - 2, -1, -1):
        out = jnp.where(code == k, jnp.int32(values[k]), out)
    return out


def seam_steps(so, t, n):
    north = lax.rem(so[0, t] - t + GW + n, n)
    south = lax.rem(t + GW - so[2, t] + n, n)
    return north, south


def wanted_rim(slot, t, so, sf, cf, n):
    north, south = seam_steps(so, t, n)
    if slot == 0:
        return sf[3, t]
    if slot == 1:
        return sf[1, t]
    if slot == 2:
        return cf[0, t]
    if slot == 3:
        return jnp.where(north == 0, sf[0, t], cf[0, t])
    if slot == 4:
        return jnp.where(north == 1, sf[0, t], cf[1, t])
    if slot == 5:
        return cf[1, t]
    if slot == 6:
        return cf[2, t]
    if slot == 7:
        return jnp.where(south == 0, sf[2, t], cf[2, t])
    if slot == 8:
        return jnp.where(south == 1, sf[2, t], cf[3, t])
    return cf[3, t]


def send_matrix(me, n, so, sf, cf):
    parts = [None] * 10
    for slot in range(10):
        rows = ROWS[slot]
        code = wanted_rim(slot, lax.rem(me - OFFSETS[slot] + n, n), so, sf, cf, n)
        a = pick(code, (0, 7, 63, 56))
        b = pick(code, (8, -1, -8, 1))
        d = pick(code, (1, 8, -1, -8))
        row = lax.broadcasted_iota(jnp.int32, (rows, 64), 0)
        pixel = lax.broadcasted_iota(jnp.int32, (rows, 64), 1)
        if rows == 32:
            i, j = row >> 3, row & 7
            valid = row < 24
        else:
            i, j = row >> 2, row & 3
            valid = (row < 12) & (j < 3)
        hit = (pixel == a + b * i + d * j) & valid
        parts[slot] = jnp.where(hit, 1.0, 0.0).astype(F32)
    order = sorted(range(10), key=lambda s: BASE[s])
    return jnp.concatenate([parts[s] for s in order], axis=0)


def place_matrix(me, n, so, cl):
    north, south = seam_steps(so, me, n)
    nz, sz = north == 0, south == 0

    def base(zero, slot_a, slot_b):
        return jnp.where(zero, jnp.int32(BASE[slot_a]), jnp.int32(BASE[slot_b]))

    def step(zero, slot_a, slot_b):
        return jnp.where(
            zero, jnp.int32(8 if ROWS[slot_a] == 32 else 4), jnp.int32(8 if ROWS[slot_b] == 32 else 4)
        )

    x = lax.broadcasted_iota(jnp.int32, (16, 256), 0)
    lane = lax.broadcasted_iota(jnp.int32, (16, 256), 1)
    live = [cl[c, me] == 1 for c in range(4)]

    def corner(c, i, j):
        zero, sa, sb = ((nz, 2, 3), (nz, 4, 5), (sz, 6, 7), (sz, 8, 9))[c]
        col = base(zero, sa, sb) + i * step(zero, sa, sb) + j
        return jnp.where(live[c], col, -1)

    blocks = []
    for y in range(14):
        if y < 3:
            left = corner(0, 2 - y, 2 - x)
            mid = base(nz, 3, 4) + (2 - y) * 8 + 10 - x
            right = corner(1, x - 11, 2 - y)
        elif y < 11:
            left = BASE[0] + (2 - x) * 8 + y - 3
            mid = jnp.full_like(x, -1)
            right = BASE[1] + (x - 11) * 8 + 10 - y
        else:
            left = corner(3, 2 - x, y - 11)
            mid = base(sz, 7, 8) + (y - 11) * 8 + x - 3
            right = corner(2, y - 11, x - 11)
        col = jnp.where(x < 3, left, jnp.where(x < 11, mid, jnp.where(x < 14, right, -1)))
        blocks.append(jnp.where(lane == col, 1.0, 0.0).astype(F32))
    blocks.append(jnp.zeros((32, 256), F32))
    return jnp.concatenate(blocks, axis=0)


def whole_wait(ref, sem):
    pltpu.make_async_copy(ref, ref, sem).wait()


def kernel(
    n,
    xin, cot, so_in, sf_in, cf_in, cl_in, dk_in, ng_in, ls_in, win_in, wout_in,
    dx_out, gin_out, gout_out, small_s,
    r1, g2, r2, g3, r3, ag, sm, sr0, s0, sr1, s1, sr2, s2, sr3, s3,
    so, sf, cf, cl, x_s, x0_s, cot_s, s0_m, dk_s, ng_s, ls_s,
    win, wout, win_t, wout_t, pk, s_m, st_m, p_m, pt_m,
    pad, dpad, normed_s, inv_s, mixed_s, before_s, slope_s,
    u_s, h_s, dm_s, db_s, a_s, b_s,
    send_f, recv_f, send_b, recv_b,
    wsem, wsend, pksem, fs_sem, fr_sem, bs_sem, br_sem, psend, precv,
    ms_sem, mr_sem, go_sem, ss_sem, sr_sem, so_sem, in_sem, xr_sem, gp_sem,
):
    seg = lax.axis_index("segment")
    me = lax.axis_index("tile")
    other = 1 - seg

    seams = [
        pltpu.make_async_copy(src, dst, in_sem.at[k])
        for k, (src, dst) in enumerate(((so_in, so), (sf_in, sf), (cf_in, cf), (cl_in, cl)))
    ]
    x_copy = pltpu.make_async_copy(xin.at[seg], x_s, in_sem.at[4])
    small_in = [
        pltpu.make_async_copy(src, dst, in_sem.at[5 + k])
        for k, (src, dst) in enumerate(((dk_in, dk_s), (ng_in, ng_s), (ls_in, ls_s)))
    ]
    for copy in [*seams, x_copy, *small_in]:
        copy.start()

    z = lax.rem(me, NZ)
    y = lax.rem(me // NZ, NY)
    x = me // (NZ * NY)
    at1, at2 = x + seg * (y - x), y + seg * (x - y)
    stride1 = NY * NZ - seg * (NY * NZ - NZ)
    stride2 = NZ + seg * (NY * NZ - NZ)

    def device_of(t):
        row = t // NZ
        hi = row // NY
        lo = row - hi * NY
        lo = lo + lax.rem(hi, 2) * (NY - 1 - 2 * lo)
        return (hi * NY + lo) * NZ + lax.rem(t, NZ)

    odd = lax.rem(x, 2)
    tile = device_of(me)
    mirror = tile

    def peer1(d):
        to = lax.rem(at1 + d, NX)
        return to, me + (to - at1) * stride1

    def peer2(d):
        to = lax.rem(at2 + d, NX)
        return to, me + (to - at2) * stride2

    def peer3(d):
        to = lax.rem(z + d, NZ)
        return to, me + to - z

    barrier = pltpu.get_barrier_semaphore()
    partners = [(seg, peer1(d)[1]) for d in range(1, NX)]
    partners += [(other, peer1(d)[1]) for d in range(1, NX)]
    partners += [(seg, peer2(d)[1]) for d in range(1, NX)]
    partners += [(other, peer2(d)[1]) for d in range(1, NX)]
    partners += [(seg, peer3(d)[1]) for d in range(1, NZ)]
    for off in OFFSETS:
        if abs(off) not in (NZ, 3 * NZ):
            partners.append((seg, lax.rem(tile + off + n, n)))
        partners.append((seg, device_of(lax.rem(tile + off + n, n))))
    partners.append((other, me))
    for partner in partners:
        pl.semaphore_signal(barrier, inc=1, device_id=partner, device_id_type=MESH)

    @pl.when(odd == 1)
    def _():
        pl.semaphore_signal(barrier, inc=1, device_id=(seg, mirror), device_id_type=MESH)

    stays = {off: tile == lax.rem(me - off + n, n) for off in OFFSETS if abs(off) in (NZ, 3 * NZ)}
    signals = len(partners) + odd
    for off, stay in stays.items():
        signals = signals + jnp.where(stay, 0, 1)

        @pl.when(jnp.logical_not(stay))
        def _():
            pl.semaphore_signal(
                barrier, inc=1, device_id=(seg, lax.rem(tile + off + n, n)), device_id_type=MESH
            )

    mine = pl.ds(2 * seg, 2)
    for l in range(2):
        b = 2 * seg + l
        pltpu.make_async_copy(win_in.at[l], win.at[b], wsem.at[0, b]).start()
        pltpu.make_async_copy(wout_in.at[l], wout.at[b], wsem.at[1, b]).start()

    for copy in seams:
        copy.wait()
    s0_m[...] = send_matrix(me, n, so, sf, cf).astype(BF16)
    x_copy.wait()
    send_f[0] = dot(s0_m[...], x_s[...]).astype(BF16)

    for copy in small_in:
        copy.wait()
    taps = dk_s[...].astype(F32)
    for l in range(2):
        b = 2 * seg + l
        pk[b, 0:49, :] = taps[:, l, :]
        pk[b, 49:50, :] = ng_s[l : l + 1, :]
        pk[b, 50:51, :] = ls_s[l : l + 1, :]
        pk[b, 51:64, :] = jnp.zeros((13, C), F32)

    pl.semaphore_wait(barrier, signals)

    first = [device_of(lax.rem(me - off + n, n)) for off in OFFSETS]
    behind = [device_of(lax.rem(tile - off + n, n)) for off in OFFSETS]
    ahead = [device_of(lax.rem(tile + off + n, n)) for off in OFFSETS]

    def exchange(src, dst, ssem, rsem, sign, home):
        for slot in SEND_ORDER:
            off = OFFSETS[slot]
            rows = pl.ds(BASE[slot], ROWS[slot])

            to = ahead[slot] if sign < 0 else behind[slot] if home is tile else first[slot]

            def go():
                pltpu.make_async_remote_copy(
                    src_ref=src.at[rows],
                    dst_ref=dst.at[rows],
                    send_sem=ssem,
                    recv_sem=rsem,
                    device_id=(seg, to),
                    device_id_type=MESH,
                ).start()

            if home is tile or off not in stays:
                go()
            else:
                pl.when(jnp.logical_not(stays[off]))(go)

                @pl.when(stays[off])
                def _():
                    pltpu.make_async_copy(src.at[rows], dst.at[rows], rsem).start()

    def to_partner(src, dst, ssem, rsem):
        return pltpu.make_async_remote_copy(
            src_ref=src, dst_ref=dst, send_sem=ssem, recv_sem=rsem,
            device_id=(other, me), device_id_type=MESH,
        )

    exchange(send_f.at[0], recv_f.at[0], fs_sem.at[0], fr_sem.at[0], 1, me)

    @pl.when(odd == 1)
    def _():
        for k, (src, dst) in enumerate(((xin, x0_s), (cot, cot_s))):
            pltpu.make_async_remote_copy(
                src_ref=src.at[seg], dst_ref=dst, send_sem=xr_sem.at[0, k], recv_sem=xr_sem.at[1, k],
                device_id=(seg, mirror), device_id_type=MESH,
            ).start()

    @pl.when(odd == 0)
    def _():
        for k, (src, dst) in enumerate(((xin, x0_s), (cot, cot_s))):
            pltpu.make_async_copy(src.at[seg], dst, xr_sem.at[1, k]).start()

    pk_copy = to_partner(pk.at[mine], pk.at[mine], pksem.at[0], pksem.at[1])
    pk_copy.start()
    def operands(b, which):
        src, dst = ((u_s, h_s), (dm_s, db_s))[which], (a_s, b_s)[which]
        for kind in range(2):
            at = (x, y)[kind]
            whole = (kind == 0) == (which == 0)
            for d in range(NX):
                to = lax.rem(at + d, NX)
                t = me + (to - at) * (NY * NZ, NZ)[kind]
                part = src[0].at[b] if whole else src[1].at[b, to]
                slot = dst.at[b, 2 * at + seg]

                def go():
                    send(part, slot, psend.at[which, b], precv.at[which, b], (kind, t))

                if d > 0:
                    go()
                else:
                    pl.when(seg != kind)(go)

                    @pl.when(seg == kind)
                    def _():
                        pltpu.make_async_copy(part, slot, precv.at[which, b]).start()

    def send(src, dst, ssem, rsem, device):
        pltpu.make_async_remote_copy(
            src_ref=src, dst_ref=dst, send_sem=ssem, recv_sem=rsem,
            device_id=device, device_id_type=MESH,
        ).start()

    w_copies = []
    for l in range(2):
        b = 2 * seg + l
        w_copies.append(to_partner(win_in.at[l], win.at[b], wsend.at[0, l], wsem.at[0, b]))
        w_copies.append(to_partner(wout_in.at[l], wout.at[b], wsend.at[1, l], wsem.at[1, b]))
    for copy in w_copies:
        copy.start()

    s_f = send_matrix(tile, n, so, sf, cf)
    s_m[...] = s_f.astype(BF16)
    st_m[...] = jnp.transpose(s_f).astype(BF16)
    p_f = place_matrix(tile, n, so, cl)
    p_m[...] = p_f.astype(BF16)
    pt_m[...] = jnp.transpose(p_f).astype(BF16)
    pk_copy.wait()
    whole_wait(x0_s, xr_sem.at[1, 0])
    curb = x0_s[...]

    q1, q2, q3 = 2048 // NX, 2048 // NX // NX, 2048 // NX // NX // NZ
    w1 = 64 // NX

    def deliver(b, block):
        l, owner = b % 2, b // 2
        row = pl.multiple_of(lax.rem(block, 2) * 128, 128)
        column = pl.multiple_of((block // 2) * 128, 128)
        base = pl.multiple_of(at1 * C, 128)
        src = ag.at[b, pl.ds(block * q2, q2)]
        for kind in range(2):

            @pl.when(seg == kind)
            def _():
                if kind == 0:
                    dst = gin_out.at[l, pl.ds(row, 128), pl.ds(base + column, 128)]
                else:
                    dst = gout_out.at[l, pl.ds(base + row, 128), pl.ds(column, 128)]
                for d in range(1, NX):
                    send(src, dst, ms_sem.at[5, b], go_sem.at[l, kind], (owner, peer1(d)[1]))
                if kind == owner:
                    pltpu.make_async_copy(src, dst, go_sem.at[l, kind]).start()
                else:
                    send(src, dst, ms_sem.at[6, b], go_sem.at[l, kind], (other, me))

    def main_chain(b):
        l, owner = b % 2, b // 2
        yield
        for which, ref in ((0, a_s), (1, b_s)):
            whole_wait(ref.at[b], precv.at[which, b])
        total = dot(a_s[b].reshape(128 * NX, C), b_s[b].reshape(128 * NX, C), 0, 0)
        for j in range(2):
            g2[b, C * j : C * j + C, :] = total[:, 128 * j : 128 * j + 128].astype(BF16)
        for d in range(1, NX):
            to, t = peer2(d)
            send(g2.at[b, pl.ds(to * q2, q2)], r2.at[b, d - 1], ms_sem.at[1, b], mr_sem.at[1, b], (seg, t))
        yield
        whole_wait(r2.at[b], mr_sem.at[1, b])
        total = g2[b, pl.ds(at2 * q2, q2), :].astype(F32)
        for d in range(NX - 1):
            total = total + r2[b, d].astype(F32)
        g3[b] = total.astype(BF16)
        here2 = pl.ds(at2 * q2, q2)
        for d in range(1, NZ):
            to, t = peer3(d)
            send(g3.at[b, pl.ds(to * q3, q3)], r3.at[b, d - 1], ms_sem.at[2, b], mr_sem.at[2, b], (seg, t))
        yield
        whole_wait(r3.at[b], mr_sem.at[2, b])
        total = g3[b, pl.ds(z * q3, q3), :].astype(F32)
        for d in range(NZ - 1):
            total = total + r3[b, d].astype(F32)
        here = pl.ds(at2 * q2 + z * q3, q3)
        ag[b, here, :] = total.astype(BF16)
        for d in range(1, NZ):
            send(ag.at[b, here], ag.at[b, here], ms_sem.at[3, b], mr_sem.at[3, b], (seg, peer3(d)[1]))
        yield
        whole_wait(ag.at[b, pl.ds(0, (NZ - 1) * q3)], mr_sem.at[3, b])
        for d in range(1, NX):
            arrived = gp_sem.at[d - 1] if b == 0 else mr_sem.at[4, b]
            send(ag.at[b, here2], ag.at[b, here2], ms_sem.at[4, b], arrived, (seg, peer2(d)[1]))
        if b == 0:
            deliver(b, at2)
        yield
        if b == 0:
            for d in (1, 3, 2):
                block = lax.rem(at2 - d + NX, NX)
                whole_wait(ag.at[b, pl.ds(block * q2, q2)], gp_sem.at[d - 1])
                deliver(b, block)
            return
        whole_wait(ag.at[b, pl.ds(0, (NX - 1) * q2)], mr_sem.at[4, b])
        for kind in range(2):

            @pl.when(seg == kind)
            def _():
                at = pl.multiple_of(at1 * C, 128)
                pairs = []
                for j in range(2):
                    if kind == 0:
                        dst = gin_out.at[l, :, pl.ds(at + 128 * j, 128)]
                    else:
                        dst = gout_out.at[l, pl.ds(at, C), pl.ds(128 * j, 128)]
                    pairs.append((ag.at[b, pl.ds(C * j, C)], dst))
                for d in range(1, NX):
                    for src, dst in pairs:
                        send(src, dst, ms_sem.at[5, b], go_sem.at[l, kind], (owner, peer1(d)[1]))
                for src, dst in pairs:
                    if kind == owner:
                        pltpu.make_async_copy(src, dst, go_sem.at[l, kind]).start()
                    else:
                        send(src, dst, ms_sem.at[6, b], go_sem.at[l, kind], (other, me))

    def small_chain(b):
        l, owner = b % 2, b // 2
        send(sm.at[b, pl.ds(other * 64, 64)], sr0.at[b], ss_sem.at[0, b], sr_sem.at[0, b], (other, me))
        yield
        whole_wait(sr0.at[b], sr_sem.at[0, b])
        s0[b] = sm[b, pl.ds(seg * 64, 64), :] + sr0[b]
        for d in range(1, NX):
            to, t = peer1(d)
            send(s0.at[b, pl.ds(to * w1, w1)], sr1.at[b, d - 1], ss_sem.at[1, b], sr_sem.at[1, b], (seg, t))
        yield
        whole_wait(sr1.at[b], sr_sem.at[1, b])
        s1[b] = s0[b, pl.ds(at1 * w1, w1), :] + jnp.sum(sr1[b], axis=0)
        for d in range(1, NX):
            send(s1.at[b], sr2.at[b, d - 1], ss_sem.at[2, b], sr_sem.at[2, b], (seg, peer2(d)[1]))
        yield
        whole_wait(sr2.at[b], sr_sem.at[2, b])
        s2[b] = s1[b] + jnp.sum(sr2[b], axis=0)
        for d in range(1, NZ):
            send(s2.at[b], sr3.at[b, d - 1], ss_sem.at[3, b], sr_sem.at[3, b], (seg, peer3(d)[1]))
        yield
        whole_wait(sr3.at[b], sr_sem.at[3, b])
        s3[b] = s2[b] + jnp.sum(sr3[b], axis=0)
        out = small_s.at[l, pl.ds(seg * 64 + at1 * w1, w1)]
        for d in range(1, NX):
            send(s3.at[b], out, ss_sem.at[4, b], so_sem.at[l], (owner, peer1(d)[1]))

        @pl.when(seg == owner)
        def _():
            pltpu.make_async_copy(s3.at[b], out, so_sem.at[l]).start()

        @pl.when(seg != owner)
        def _():
            send(s3.at[b], out, ss_sem.at[5, b], so_sem.at[l], (other, me))

    chains = []

    def begin(chain):
        next(chain)
        chains.append(chain)

    def advance(which=None):
        for chain in list(chains if which is None else which):
            if chain in chains and next(chain, True):
                chains.remove(chain)

    def slope_of(b):
        before = before_s[...]
        slope_s[b] = (
            0.5 * (1.0 + lax.erf(before * ROOT_HALF))
            + before * jnp.exp(-0.5 * before * before) * INV_ROOT_TAU
        )

    def turn(b):
        win_t[b] = jnp.transpose(win[b])
        wout_t[b] = jnp.transpose(wout[b])

    for b in range(BLOCKS):
        if b > 0:
            send_f[b] = dot(s_m[...], curb).astype(BF16)
            exchange(send_f.at[b], recv_f.at[b], fs_sem.at[b], fr_sem.at[b], 1, tile)
            slope_of(b - 1)
            turn(b - 1)
        cur = curb.astype(F32)
        whole_wait(recv_f.at[b], fr_sem.at[b])
        pad[b] = dot(p_m[...], recv_f[b]).reshape(16, 16, C)
        pad[b, 3:11, 3:11, :] = cur.reshape(8, 8, C)
        acc = jnp.zeros((8, 8, C), F32)
        for q in range(7):
            cols = pad[b, 0:14, q : q + 8, :]
            for r in range(7):
                acc = acc + cols[r : r + 8] * pk[b, 7 * r + q : 7 * r + q + 1, :]
        filtered = acc.reshape(64, C)
        centred = filtered - jnp.mean(filtered, axis=-1, keepdims=True)
        inv_std = lax.rsqrt(jnp.mean(centred * centred, axis=-1, keepdims=True) + EPSILON)
        normed = centred * inv_std
        normed_s[b] = normed
        inv_s[b] = jnp.broadcast_to(inv_std, (64, 128))
        unit = (normed * pk[b, 49:50, :]).astype(BF16)
        u_s[b] = unit
        whole_wait(win.at[b], wsem.at[0, b])
        before = dot(unit, win[b])
        before_s[...] = before
        hidden = (0.5 * before * (1.0 + lax.erf(before * ROOT_HALF))).astype(BF16)
        for k in range(NX):
            h_s[b, k] = hidden[:, k * HID // NX : (k + 1) * HID // NX]
        whole_wait(wout.at[b], wsem.at[1, b])
        mixed = dot(hidden, wout[b])
        mixed_s[b] = mixed
        curb = (cur + pk[b, 50:51, :] * mixed).astype(BF16)

        operands(b, 0)

    whole_wait(cot_s, xr_sem.at[1, 1])
    up = cot_s[...].astype(F32)
    slope_of(BLOCKS - 1)
    for b in reversed(range(BLOCKS)):
        dm = (up * pk[b, 50:51, :]).astype(BF16)
        dm_s[b] = dm

        d_hidden = dot(dm, wout_t[b]) if b < BLOCKS - 1 else dot(dm, wout[b], 1, 1)
        db = (d_hidden * slope_s[b]).astype(BF16)
        for k in range(NX):
            db_s[b, k] = db[:, k * HID // NX : (k + 1) * HID // NX]
        if b == 0:
            operands(b, 1)
        d_unit = dot(db, win_t[b]) if b < BLOCKS - 1 else dot(db, win[b], 1, 1)
        normed = normed_s[b]
        inv_std = inv_s[b, :, 0:1]
        dn = d_unit * pk[b, 49:50, :]
        df = inv_std * (
            dn
            - jnp.mean(dn, axis=-1, keepdims=True)
            - normed * jnp.mean(dn * normed, axis=-1, keepdims=True)
        )
        df = df.reshape(8, 8, C)
        older = list(chains)

        def put(row, value):
            sm[b, row : row + 1, :] = value[:, 0:128]
            sm[b, 64 + row : 65 + row, :] = value[:, 128:256]

        def small_grads():
            put(49, jnp.sum(d_unit * normed, axis=0, keepdims=True))
            put(50, jnp.sum(up * mixed_s[b], axis=0, keepdims=True))
            sm[b, 51:64, :] = jnp.zeros((13, 128), F32)
            sm[b, 115:128, :] = jnp.zeros((13, 128), F32)
            for q in range(7):
                cols = pad[b, 0:14, q : q + 8, :]
                for r in range(7):
                    tap = 7 * r + q
                    prod = jnp.sum(df * cols[r : r + 8], axis=0)
                    put(tap, jnp.sum(prod, axis=0, keepdims=True))
            begin(small_chain(b))

        begin(main_chain(b))

        if b == 0:
            small_grads()
        dpad[...] = jnp.zeros((16, 16, C), F32)
        for q in range(7):
            rows = [None] * 14
            for r in range(7):
                term = df * pk[b, 7 * r + q : 7 * r + q + 1, :]
                for i in range(8):
                    part = term[i]
                    rows[r + i] = part if rows[r + i] is None else rows[r + i] + part
            dpad[0:14, q : q + 8, :] += jnp.stack(rows)
        send_b[b] = dot(pt_m[...], dpad[...].reshape(256, C).astype(BF16)).astype(BF16)
        exchange(send_b.at[b], recv_b.at[b], bs_sem.at[b], br_sem.at[b], -1, tile)

        if b > 0:
            operands(b, 1)
        advance(older)
        if b > 0:
            small_grads()
        whole_wait(recv_b.at[b], br_sem.at[b])
        back = dot(st_m[...], recv_b[b])
        up = (up + dpad[3:11, 3:11, :].reshape(64, C) + back).astype(BF16)
        if b == 0:
            x_s[...] = up

            @pl.when(odd == 1)
            def _():
                pltpu.make_async_remote_copy(
                    src_ref=x_s, dst_ref=dx_out, send_sem=xr_sem.at[0, 2], recv_sem=xr_sem.at[1, 2],
                    device_id=(seg, mirror), device_id_type=MESH,
                ).start()

            @pl.when(odd == 0)
            def _():
                pltpu.make_async_copy(x_s, dx_out, xr_sem.at[1, 2]).start()

        up = up.astype(F32)

    while chains:
        advance(chains[::-1])
    for l in range(2):
        whole_wait(small_s.at[l], so_sem.at[l])
        whole_wait(gin_out.at[l], go_sem.at[l, 0])
        whole_wait(gout_out.at[l], go_sem.at[l, 1])
    whole_wait(dx_out, xr_sem.at[1, 2])
    stay = functools.reduce(jnp.logical_or, stays.values())
    kept = 256 - ROWS[OFFSETS.index(next(iter(stays)))]

    @pl.when(stay)
    def _():
        whole_wait(send_f.at[0, pl.ds(0, kept)], fs_sem.at[0])

    @pl.when(jnp.logical_not(stay))
    def _():
        whole_wait(send_f.at[0], fs_sem.at[0])

    @pl.when(odd == 1)
    def _():
        for k in range(3):
            whole_wait(x_s, xr_sem.at[0, k])

    for copy in w_copies:
        copy.wait_send()
    for b in range(BLOCKS):
        if b > 0:
            whole_wait(send_f.at[b], fs_sem.at[b])
        whole_wait(send_b.at[b], bs_sem.at[b])
        for which in range(2):
            whole_wait(a_s.at[b, pl.ds(0, 2 * NX - 1)], psend.at[which, b])
        whole_wait(r2.at[b], ms_sem.at[1, b])
        whole_wait(r3.at[b], ms_sem.at[2, b])
        whole_wait(r3.at[b], ms_sem.at[3, b])
        whole_wait(r2.at[b], ms_sem.at[4, b])
        whole_wait(r1.at[b], ms_sem.at[5, b])
        whole_wait(sr0.at[b], ss_sem.at[0, b])
        whole_wait(sr1.at[b], ss_sem.at[1, b])
        whole_wait(sr2.at[b], ss_sem.at[2, b])
        whole_wait(sr3.at[b], ss_sem.at[3, b])
        whole_wait(sr1.at[b], ss_sem.at[4, b])

        @pl.when(seg != b // 2)
        def _():
            whole_wait(ag.at[b], ms_sem.at[6, b])
            whole_wait(s3.at[b], ss_sem.at[5, b])


def finish(
    factor, dx, gin, gout, small, dx_out, gin_out, gout_out, gk_out, gg_out, gs_out,
    in_n, in_w, out_n, out_w, small_n, gk_w, gg_w, gs_w, in_sem, out_sem,
):
    loads, stores, stages = [], [], []
    for src, dst, narrow, wide in ((gin, gin_out, in_n, in_w), (gout, gout_out, out_n, out_w)):
        rows = src.shape[1] // 2
        for l in range(2):
            for h in range(2):
                part = pl.ds(h * rows, rows)
                k = len(loads)
                loads.append(pltpu.make_async_copy(src.at[l, part], narrow.at[l, part], in_sem.at[k]))
                stores.append(pltpu.make_async_copy(wide.at[l, part], dst.at[l, part], out_sem.at[k]))
                stages.append((narrow, wide, l, part))
    first = pltpu.make_async_copy(small, small_n, in_sem.at[8])
    pass_on = pltpu.make_async_copy(dx, dx_out, in_sem.at[9])
    for load in (*loads[:1], first, *loads[1:], pass_on):
        load.start()
    for load, store, (narrow, wide, l, part) in zip(loads, stores, stages):
        load.wait()
        wide[l, part] = narrow[l, part].astype(F32) * factor
        store.start()
    first.wait()
    for l in range(2):
        total = jnp.concatenate([small_n[l, 0:64, :], small_n[l, 64:128, :]], axis=1) * factor
        gk_w[:, l, :] = total[0:49]
        gg_w[l : l + 1, :] = total[49:50]
        gs_w[l : l + 1, :] = total[50:51]
    last = [
        pltpu.make_async_copy(src, dst, out_sem.at[8 + k])
        for k, (src, dst) in enumerate(((gk_w, gk_out), (gg_w, gg_out), (gs_w, gs_out)))
    ]
    for copy in last:
        copy.start()
    for copy in (*stores, *last, pass_on):
        copy.wait()


def local(
    inputs, cotangent, side_owner, side_from, corner_from, corner_live,
    depth_kernel, norm_gain, in_weight, out_weight, layer_scale,
):
    n = lax.axis_size("tile")
    factor = (2 * n * 64) ** (-0.5)
    vmem = pl.BlockSpec(memory_space=pltpu.VMEM)
    hbm = pl.BlockSpec(memory_space=pl.ANY)
    V = pltpu.VMEM
    S = pltpu.SMEM
    shape = jax.ShapeDtypeStruct
    q1, q2, q3 = 2048 // NX, 2048 // NX // NX, 2048 // NX // NX // NZ
    w1 = 64 // NX
    dma = pltpu.SemaphoreType.DMA
    dx, d_in, d_out, small = pl.pallas_call(
        functools.partial(kernel, n),
        out_shape=(
            shape((64, C), BF16), shape((2, C, HID), BF16), shape((2, HID, C), BF16), shape((2, 128, 128), F32),
        ),
        in_specs=[hbm] * 11,
        out_specs=(hbm,) * 4,
        scratch_shapes=[
            V((BLOCKS, NX - 1, q1, 128), BF16), V((BLOCKS, q1, 128), BF16),
            V((BLOCKS, NX - 1, q2, 128), BF16), V((BLOCKS, q2, 128), BF16), V((BLOCKS, NZ - 1, q3, 128), BF16),
            V((BLOCKS, q1, 128), BF16), V((BLOCKS, 128, 128), F32),
            V((BLOCKS, 64, 128), F32), V((BLOCKS, 64, 128), F32),
            V((BLOCKS, NX - 1, w1, 128), F32), V((BLOCKS, w1, 128), F32),
            V((BLOCKS, NX - 1, w1, 128), F32), V((BLOCKS, w1, 128), F32),
            V((BLOCKS, NZ - 1, w1, 128), F32), V((BLOCKS, w1, 128), F32),
            S((4, n), jnp.int32), S((4, n), jnp.int32), S((4, n), jnp.int32), S((4, n), jnp.int32),
            V((64, C), BF16), V((64, C), BF16), V((64, C), BF16), V((256, 64), BF16),
            V((49, 2, C), BF16), V((2, C), F32), V((2, C), F32),
            V((BLOCKS, C, HID), BF16), V((BLOCKS, HID, C), BF16),
            V((BLOCKS - 1, HID, C), BF16), V((BLOCKS - 1, C, HID), BF16), V((BLOCKS, SMALL, C), F32),
            V((256, 64), BF16), V((64, 256), BF16), V((256, 256), BF16), V((256, 256), BF16),
            V((BLOCKS, 16, 16, C), F32), V((16, 16, C), F32),
            V((BLOCKS, 64, C), F32), V((BLOCKS, 64, 128), F32), V((BLOCKS, 64, C), F32),
            V((64, HID), F32), V((BLOCKS, 64, HID), F32),
            V((BLOCKS, 64, C), BF16), V((BLOCKS, NX, 64, HID // NX), BF16),
            V((BLOCKS, 64, C), BF16), V((BLOCKS, NX, 64, HID // NX), BF16),
            V((BLOCKS, 2 * NX, 64, C), BF16), V((BLOCKS, 2 * NX, 64, C), BF16),
            V((BLOCKS, 256, C), BF16), V((BLOCKS, 256, C), BF16),
            V((BLOCKS, 256, C), BF16), V((BLOCKS, 256, C), BF16),
            dma((2, BLOCKS)), dma((2, 2)), dma((2,)),
            dma((BLOCKS,)), dma((BLOCKS,)), dma((BLOCKS,)), dma((BLOCKS,)),
            dma((2, BLOCKS)), dma((2, BLOCKS)),
            dma((7, BLOCKS)), dma((5, BLOCKS)), dma((2, 2)), dma((6, BLOCKS)), dma((4, BLOCKS)), dma((2,)),
            dma((8,)), dma((2, 3)), dma((3,)),
        ],
        compiler_params=pltpu.CompilerParams(
            collective_id=0, has_side_effects=True, vmem_limit_bytes=VMEM_BYTES
        ),
    )(
        inputs.reshape(2, 64, C), cotangent.reshape(2, 64, C),
        side_owner.T, side_from.T, corner_from.T, corner_live.T,
        depth_kernel.transpose(1, 0, 2), norm_gain, layer_scale, in_weight, out_weight,
    )
    dx, d_in, d_out, d_kernel, d_gain, d_scale = pl.pallas_call(
        functools.partial(finish, factor),
        out_shape=(
            shape((1, 8, 8, C), BF16), shape((2, C, HID), F32), shape((2, HID, C), F32),
            shape((49, 2, C), F32), shape((2, C), F32), shape((2, C), F32),
        ),
        in_specs=[hbm] * 4,
        out_specs=(hbm,) * 6,
        scratch_shapes=[
            V((2, C, HID), BF16), V((2, C, HID), F32), V((2, HID, C), BF16), V((2, HID, C), F32),
            V((2, 128, 128), F32), V((49, 2, C), F32), V((2, C), F32), V((2, C), F32),
            dma((10,)), dma((11,)),
        ],
        compiler_params=pltpu.CompilerParams(vmem_limit_bytes=VMEM_BYTES),
    )(dx.reshape(1, 8, 8, C), d_in, d_out, small)
    return dx, d_kernel.transpose(1, 0, 2), d_gain, d_in, d_out, d_scale


def solution(mesh):
    in_specs = (
        P(None, "tile", None, None), P(None, "tile", None, None),
        P(), P(), P(), P(),
        P("segment", None, None), P("segment", None), P("segment", None, None),
        P("segment", None, None), P("segment", None),
    )
    out_specs = (
        P("segment", "tile", None, None), P("segment", None, None), P("segment", None),
        P("segment", None, None), P("segment", None, None), P("segment", None),
    )
    return jax.shard_map(local, mesh=mesh, in_specs=in_specs, out_specs=out_specs, check_vma=False)
```
